512 devices in a mesh: gx: 16 (over z), gy: 8 (over y, core), gz: 4 (over x).
Axes of the slice: x: 4, y: 4, z: 16, core: 2. Of those that a mesh axis runs over, the one named last changes fastest.
Arguments:
- rhs: float32 [256, 256, 512], P('gx', 'gy', 'gz'), may hold values from -8 to 8
- kappa: float32 [256, 256, 512], P('gx', 'gy', 'gz'), may hold values from 0.1 to 10
Outputs:
- pressure: float32 [256, 256, 512], P('gx', 'gy', 'gz')
- residual: float32 [256, 256, 512], P('gx', 'gy', 'gz')
The draws below stay inside these ranges and needn't reach their ends.
All inputs are finite; a program needn't handle non-finite values.
Results may differ from the reference program's by a relative error of at most 0.0003.
Values sent between devices are 32-bit elements; how exact they have to be, the bound alone decides.
A program may use at most 128 MiB of HBM per device.

```python
import math
import jax
import jax.numpy as jnp

COARSE_SWEEPS = 8
NX = 256
NY = 256
NZ = 512


def shard_levels(rng, extent, split, low, high):
    gain = 1.0
    for position, blocks in split:
        steps = jax.random.uniform(jax.random.fold_in(jax.random.fold_in(rng, 6), position), (blocks,), jnp.float32, low / len(split), high / len(split))
        gain = gain * jnp.repeat(jnp.exp(steps), extent[position] // blocks).reshape((-1,) + (1,) * (len(extent) - 1 - position))
    return gain


def centred(rng, extent, width, limit, cuts=(), kind=jnp.bfloat16):
    drawn = width * jax.random.normal(rng, extent, jnp.float32)
    if cuts:
        drawn = drawn * shard_levels(rng, extent, cuts, -0.22, 0.18)
    return jnp.clip(drawn, -limit, limit).astype(kind)


def setup_inputs(seed: int = 0) -> dict:
    streams_of = jax.random.split(jax.random.key(seed), 3)
    rhs = centred(streams_of[0], (NX, NY, NZ), 1.0, 8.0, ((0, 16), (1, 8), (2, 4)), jnp.float32)
    kappa = jnp.clip(jnp.exp(math.log(10.0) - 4.6051702 * jax.random.uniform(streams_of[1], (NX, NY, NZ), jnp.float32) ** shard_levels(streams_of[1], (NX, NY, NZ), ((0, 16), (1, 8), (2, 4)), -0.2, 0.2)), 0.1, 10.0)
    return {"rhs": rhs, "kappa": kappa}


OMEGA = 0.8


def neighbours(padded):
    return [padded[:-2, 1:-1, 1:-1], padded[2:, 1:-1, 1:-1],
            padded[1:-1, :-2, 1:-1], padded[1:-1, 2:, 1:-1],
            padded[1:-1, 1:-1, :-2], padded[1:-1, 1:-1, 2:]]


def face_weights(kappa_padded, scale):
    centre = kappa_padded[1:-1, 1:-1, 1:-1]
    weights = [scale * 0.5 * (centre + other) for other in neighbours(kappa_padded)]
    diag = weights[0] + weights[1] + weights[2] + weights[3] + weights[4] + weights[5]
    return weights, diag


def apply_padded(field, padded, weights, diag):
    others = neighbours(padded)
    total = weights[0] * others[0]
    for index in range(1, 6):
        total = total + weights[index] * others[index]
    return diag * field - total


def restrict(field):
    a, b, c = field.shape
    return field.reshape(a // 2, 2, b // 2, 2, c // 2, 2).mean(axis=(1, 3, 5))


def prolong(field):
    return jnp.repeat(jnp.repeat(jnp.repeat(field, 2, axis=0), 2, axis=1), 2, axis=2)


def reference(rhs, kappa):
    def operate(field, weights, diag):
        return apply_padded(field, jnp.pad(field, 1), weights, diag)

    def sweep(field, source, weights, diag):
        return field + OMEGA * (source - operate(field, weights, diag)) / diag

    kappas = [kappa]
    for level in range(3):
        kappas.append(restrict(kappas[-1]))
    levels = [face_weights(jnp.pad(kappas[level], 1), 0.25 ** level) for level in range(4)]
    sources = [rhs]
    iterates = []
    for level in range(3):
        weights, diag = levels[level]
        source = sources[level]
        field = OMEGA * source / diag
        field = sweep(field, source, weights, diag)
        iterates.append(field)
        sources.append(restrict(source - operate(field, weights, diag)))
    weights, diag = levels[3]
    coarse = OMEGA * sources[3] / diag
    for step in range(COARSE_SWEEPS - 1):
        coarse = sweep(coarse, sources[3], weights, diag)
    for level in (2, 1, 0):
        weights, diag = levels[level]
        field = iterates[level] + prolong(coarse)
        field = sweep(field, sources[level], weights, diag)
        field = sweep(field, sources[level], weights, diag)
        coarse = field
    weights, diag = levels[0]
    return coarse, rhs - operate(coarse, weights, diag)
```

```python
import functools
import itertools

import jax
import jax.numpy as jnp
from jax import lax
from jax.experimental import pallas as pl
from jax.experimental.pallas import tpu as pltpu
from jax.sharding import PartitionSpec as P

MESH = pl.DeviceIdType.MESH
F32 = jnp.float32
OMEGA = 0.8
COARSE_SWEEPS = 8
GX, GY, GZ = 16, 8, 4
FACES = [(-1, 0, 0), (1, 0, 0), (0, -1, 0), (0, 1, 0), (0, 0, -1), (0, 0, 1)]
NEAR = [o for o in itertools.product((-1, 0, 1), repeat=3) if o != (0, 0, 0)]
FAR = [(a, b, 0) for a in (-4, -2, 0, 2, 4) for b in (-2, 0, 2) if (a, b) != (0, 0)]
PARTNERS = NEAR + FAR
ROUNDS = 5

L1 = dict(planes=18, rows=32, px=5, py=8, n=(8, 16, 64), right=72, left=120, level=1)
L2 = dict(planes=16, rows=24, px=6, py=8, n=(4, 8, 32), right=64, left=96, level=2)
L3 = dict(planes=22, rows=24, px=10, py=10, n=(2, 4, 16), right=32, left=112, level=3)

SCRATCH = {
    "ua": (18, 48, 128), "ub": (18, 48, 128), "k0": (18, 48, 128),
    "w0": (6, 16, 32, 128), "d0": (16, 32, 128), "i0": (16, 32, 128), "h0": (16, 32, 128),
    "ys": (ROUNDS, 2, 16, 128), "zs": (ROUNDS, 8, 128),
    "rx": (ROUNDS, 2, 32, 128), "ry": (ROUNDS, 2, 16, 128), "rz": (ROUNDS, 2, 8, 128), "mz": (8, 128),
    "sum": (256, 128), "rep": (10 * 48, 128),
    "k1": (18, 32, 128), "f1": (18, 32, 128), "u1a": (18, 32, 128), "u1b": (18, 32, 128),
    "w1": (6, 18, 32, 128), "d1": (18, 32, 128), "i1": (18, 32, 128),
    "zp1": (2, 16, 128), "zb1": (2, 2, 3, 32, 128),
    "k2": (16, 24, 128), "f2": (16, 24, 128), "u2a": (16, 24, 128), "u2b": (16, 24, 128),
    "w2": (6, 16, 24, 128), "d2": (16, 24, 128), "i2": (16, 24, 128),
    "p2": (2, 2, 8, 128), "r2": (2, 27, 2, 8, 128),
    "k3": (22, 24, 128), "f3": (22, 24, 128), "u3a": (22, 24, 128), "u3b": (22, 24, 128),
    "w3": (6, 22, 24, 128), "d3": (22, 24, 128), "i3": (22, 24, 128),
    "s3": (2, 6, 8, 128), "r3": (2, 5, 3, 6, 8, 128),
}
COPIES = ROUNDS * 6 + 2 * (26 + 26 + 14)


def lanes(shape):
    return lax.broadcasted_iota(jnp.int32, shape, len(shape) - 1)


def loop(low, high, body):
    def step(i, carry):
        body(i)
        return carry
    lax.fori_loop(low, high, step, 0, unroll=True)


def dot(a, b):
    return jnp.dot(a, b, precision=lax.Precision.HIGHEST, preferred_element_type=F32)


def pool_matrix(split):
    row = lax.broadcasted_iota(jnp.int32, (128, 128), 0)
    col = lax.broadcasted_iota(jnp.int32, (128, 128), 1)
    target = jnp.where(row < split, row // 2, 64 + row // 2)
    return jnp.where(target == col, 0.125, 0.0).astype(F32)


def repeat_matrix(split):
    row = lax.broadcasted_iota(jnp.int32, (128, 128), 0)
    col = lax.broadcasted_iota(jnp.int32, (128, 128), 1)
    origin = jnp.where(col < split, col // 2, 64 + col // 2)
    return jnp.where(origin == row, 1.0, 0.0).astype(F32)


def edge_matrix():
    row = lax.broadcasted_iota(jnp.int32, (128, 128), 0)
    col = lax.broadcasted_iota(jnp.int32, (128, 128), 1)
    hit = ((row == 127) & (col == 0)) | ((row == 64) & (col == 127))
    return jnp.where(hit, 1.0, 0.0).astype(F32)


def kernel(rhs, kap, pressure, residual, *refs):
    s = dict(zip(SCRATCH, refs))
    send, recv = refs[len(SCRATCH):]
    gx, gy, gz = lax.axis_index("gx"), lax.axis_index("gy"), lax.axis_index("gz")

    def device(o):
        return (lax.rem(gx + (o[0] + GX), GX), lax.rem(gy + (o[1] + GY), GY), lax.rem(gz + (o[2] + GZ), GZ))

    def copy(src, dst, o, index):
        return pltpu.make_async_remote_copy(
            src_ref=src, dst_ref=dst, send_sem=send.at[index], recv_sem=recv.at[index],
            device_id=device(o), device_id_type=MESH)

    barrier = pltpu.get_barrier_semaphore()
    for o in PARTNERS:
        pl.semaphore_signal(barrier, inc=1, device_id=device(o), device_id_type=MESH)

    lane8 = lanes((8, 128))
    lane32 = lanes((32, 128))
    total = s["sum"]

    def faces(u, r):
        for x in range(16):
            s["ys"][r, 0, x:x + 1, :] = u[1 + x, 8:9, :]
            s["ys"][r, 1, x:x + 1, :] = u[1 + x, 39:40, :]
        packed = jnp.zeros((8, 128), F32)
        for x in range(16):
            for t in range(4):
                k = 4 * x + t
                moved = pltpu.roll(u[1 + x, 8 + 8 * t:16 + 8 * t, :], (2 * k + 1) % 128, 1)
                packed = jnp.where((lane8 >> 1) == k, moved, packed)
        s["zs"][r] = packed
        base = 6 * r
        copies = []
        for i, o in enumerate(FACES):
            low = i % 2 == 0
            side = 1 if low else 0
            if i < 2:
                src, dst = u.at[1 if low else 16, pl.ds(8, 32)], s["rx"].at[r, side]
            elif i < 4:
                src, dst = s["ys"].at[r, 0 if low else 1], s["ry"].at[r, side]
            else:
                src, dst = s["zs"].at[r], s["rz"].at[r, side]
            copies.append(copy(src, dst, o, base + i))
        for c in copies:
            c.start()
        return copies

    def land(copies, u, r):
        for c in copies:
            c.wait()
        u[0, 8:40, :] = jnp.where(gx > 0, s["rx"][r, 0], 0.0)
        u[17, 8:40, :] = jnp.where(gx < GX - 1, s["rx"][r, 1], 0.0)
        below = jnp.where(gy > 0, s["ry"][r, 0], 0.0)
        above = jnp.where(gy < GY - 1, s["ry"][r, 1], 0.0)
        for x in range(16):
            u[1 + x, 7:8, :] = below[x:x + 1]
            u[1 + x, 40:41, :] = above[x:x + 1]
        left = jnp.where(gz > 0, s["rz"][r, 0], 0.0)
        right = jnp.where(gz < GZ - 1, s["rz"][r, 1], 0.0)
        s["mz"][...] = jnp.where((lane8 & 1) == 0, left, pltpu.roll(right, 126, 1))

    def ends(x):
        packed = s["mz"][...]
        return jnp.concatenate(
            [pltpu.roll(packed, lax.rem(256 - 8 * x - 2 * t, 128), 1) for t in range(4)], axis=0)

    def around0(u, x, end):
        c = u[1 + x, 8:40, :]
        return c, [
            u[x, 8:40, :], u[2 + x, 8:40, :], u[1 + x, 7:39, :], u[1 + x, 9:41, :],
            jnp.where(lane32 == 0, end, pltpu.roll(c, 1, 1)),
            jnp.where(lane32 == 127, end, pltpu.roll(c, 127, 1))]

    def left0(u, x, end):
        c, others = around0(u, x, end)
        acc = rhs[x] - s["d0"][x] * c
        for i in range(6):
            acc = acc + s["w0"][i, x] * others[i]
        return c, acc

    def inside(lv, p):
        n, level = lv["n"], lv["level"]
        shape = (lv["rows"], 128)
        lane = lanes(shape)
        row = lax.broadcasted_iota(jnp.int32, shape, 0)
        x = gx * n[0] + (p - lv["px"])
        y = gy * n[1] + (row - lv["py"])
        z = gz * n[2] + jnp.where(lane < lv["right"], lane, lane - 128)
        ok = (lane < lv["right"]) | (lane >= lv["left"])
        ok = ok & (y >= 0) & (y < 256 >> level) & (z >= 0) & (z < 512 >> level)
        return ok & (x >= 0) & (x < 256 >> level)

    def around(u, p, rows):
        c = u[p]
        return c, [u[p - 1], u[p + 1], pltpu.roll(c, 1, 0), pltpu.roll(c, rows - 1, 0),
                   pltpu.roll(c, 1, 1), pltpu.roll(c, 127, 1)]

    def weights(lv, k, w, d, inv):
        scale = 0.5 * 0.25 ** lv["level"]

        def clear(p):
            k[p] = jnp.where(inside(lv, p), k[p], 0.0)

        row = lax.broadcasted_iota(jnp.int32, (lv["rows"], 128), 0)
        ends_y = {2: row == 0, 3: row == lv["rows"] - 1}

        def plane(p):
            c, others = around(k, p, lv["rows"])
            diag = None
            for i in range(6):
                other = jnp.where(ends_y[i], 0.0, others[i]) if i in ends_y else others[i]
                weight = scale * (c + other)
                w[i, p] = jnp.where(ends_y[i], 0.0, weight) if i in ends_y else weight
                diag = weight if diag is None else diag + weight
            d[p] = diag
            inv[p] = jnp.where(inside(lv, p), OMEGA / diag, 0.0)
        loop(0, lv["planes"], clear)
        loop(1, lv["planes"] - 1, plane)

    def rest(lv, u, f, w, d, p):
        c, others = around(u, p, lv["rows"])
        acc = f[p] - d[p] * c
        for i in range(6):
            acc = acc + w[i, p] * others[i]
        return c, acc

    def sweep(lv, u, v, f, w, d, inv, low, high):
        def plane(p):
            c, acc = rest(lv, u, f, w, d, p)
            v[p] = c + inv[p] * acc
        loop(low, high, plane)

    def first(u, f, inv, low, high):
        def plane(p):
            u[p] = f[p] * inv[p]
        loop(low, high, plane)

    def pooled_rows(count, rows, start, keep):
        parts = []
        for i in range(count):
            parts.append(total[pl.ds(rows * i + start, keep, stride=2), :]
                         + total[pl.ds(rows * i + start + 1, keep, stride=2), :])
        return jnp.concatenate(parts, axis=0)

    def sums(count, rows, plane):
        for i in range(count):
            total[rows * i:rows * i + rows, :] = plane(2 * i) + plane(2 * i + 1)

    def to_level1(plane, out, slot):
        sums(8, 32, plane)
        mean = dot(pooled_rows(8, 32, 0, 16), pool_matrix(128))
        for i in range(8):
            out[5 + i, 8:24, :] = mean[16 * i:16 * i + 16]
        lane16 = lanes((16, 128))
        packed = jnp.zeros((16, 128), F32)
        for i in range(8):
            v = mean[16 * i:16 * i + 16]
            packed = jnp.where((lane16 >= 16 * i) & (lane16 < 16 * i + 8), pltpu.roll(v, 16 * i, 1) if i else v, packed)
            packed = jnp.where((lane16 >= 16 * i + 8) & (lane16 < 16 * i + 16),
                               pltpu.roll(v, (16 * i + 8 - 56) % 128, 1), packed)
        s["zp1"][slot] = packed

    def send1(out, slot, base):
        copies = []
        for i, (a, b, c) in enumerate(NEAR):
            rows_src = {-1: (8, 8), 0: (8, 16), 1: (16, 8)}[b]
            rows_dst = {-1: 24, 0: 8, 1: 0}[b]
            if c == 0:
                first_plane, count, to = {-1: (5, 5, 13), 0: (5, 8, 5), 1: (8, 5, 0)}[a]
                src = out.at[pl.ds(first_plane, count), pl.ds(rows_src[0], rows_src[1])]
                dst = out.at[pl.ds(to, count), pl.ds(rows_dst, rows_src[1])]
            else:
                src = s["zp1"].at[slot, pl.ds(rows_src[0] - 8, rows_src[1])]
                dst = s["zb1"].at[slot, 0 if c == 1 else 1, 1 - a, pl.ds(rows_dst, rows_src[1])]
            copies.append(copy(src, dst, (a, b, c), base + i))
        for c in copies:
            c.start()
        return copies

    def land1(copies, out, slot):
        for c in copies:
            c.wait()
        for p in range(18):
            x = p - 5
            a = -1 if x < 0 else (0 if x < 8 else 1)
            q = x - 8 * a
            low = pltpu.roll(s["zb1"][slot, 0, a + 1], (120 - 16 * q - 8) % 128, 1)
            high = pltpu.roll(s["zb1"][slot, 1, a + 1], (64 - 16 * q) % 128, 1)
            out[p] = jnp.where(lane32 < 64, out[p],
                               jnp.where(lane32 < 72, high, jnp.where(lane32 >= 120, low, 0.0)))

    def to_level2(plane, first_q, count, slot):
        sums(count, 32, plane)
        rows = pooled_rows(count, 32, 8, 8)
        rows = jnp.where(lanes(rows.shape) < 64, rows, 0.0)
        mean = dot(rows, pool_matrix(128))
        packs = [jnp.zeros((8, 128), F32), jnp.zeros((8, 128), F32)]
        for i in range(count):
            q = first_q + i
            v = mean[8 * i:8 * i + 8]
            packs[q // 4] = packs[q // 4] + (pltpu.roll(v, 32 * (q % 4), 1) if q % 4 else v)
        s["p2"][slot, 0] = packs[0]
        s["p2"][slot, 1] = packs[1]

    def slot2(a, b, c):
        return 9 * (a + 1) + 3 * (b + 1) + (c + 1)

    def send2(slot, base):
        copies = []
        for i, o in enumerate(NEAR):
            copies.append(copy(s["p2"].at[slot], s["r2"].at[slot, slot2(-o[0], -o[1], -o[2])], o, base + i))
        for c in copies:
            c.start()
        s["r2"][slot, slot2(0, 0, 0)] = s["p2"][slot]
        return copies

    def land2(copies, out, slot):
        for c in copies:
            c.wait()
        for p in range(16):
            x = p - 6
            a = -1 if x < 0 else (0 if x < 4 else 1)
            q = x - 4 * a + 2

            def part(b, c, place):
                v = s["r2"][slot, slot2(a, b, c), q // 4]
                shift = (place - 32 * (q % 4)) % 128
                return pltpu.roll(v, shift, 1) if shift else v
            for b in (-1, 0, 1):
                out[p, 8 * (b + 1):8 * (b + 2), :] = jnp.where(
                    lane8 < 32, part(b, 0, 0),
                    jnp.where(lane8 < 64, part(b, 1, 32), jnp.where(lane8 >= 96, part(b, -1, 96), 0.0)))

    def to_level3(plane, slot):
        for i in range(6):
            v = plane(2 * i) + plane(2 * i + 1)
            total[40 * i:40 * i + 24, :] = v
            total[40 * i + 24:40 * i + 32, :] = v[:8]
            total[40 * i + 32:40 * i + 40, :] = v[:8]
        rows = jnp.concatenate([pooled_rows(6, 40, 4, 8), pooled_rows(6, 40, 20, 8)], axis=0)
        mean = dot(rows, pool_matrix(64))
        for i in range(6):
            more = pltpu.roll(mean[48 + 8 * i:56 + 8 * i], 48, 1)
            s["s3"][slot, i] = jnp.where((lane8 >= 32) & (lane8 < 80), more, mean[8 * i:8 * i + 8])

    def send3(slot, base):
        copies = []
        for i, (a, b, c) in enumerate(FAR):
            start, count = {0: (0, 6), 2: (0, 5), -2: (1, 5), 4: (0, 5), -4: (1, 5)}[a]
            if slot == 1 and abs(a) == 4:
                start, count = 1, 4
            copies.append(copy(
                s["s3"].at[slot, pl.ds(start, count)],
                s["r3"].at[slot, 2 - a // 2, 1 - b // 2, pl.ds(start, count)], (a, b, c), base + i))
        for c in copies:
            c.start()
        s["r3"][slot, 2, 1] = s["s3"][slot]
        return copies

    def land3(copies, out, slot, low, high):
        for c in copies:
            c.wait()
        row8 = lax.broadcasted_iota(jnp.int32, (8, 128), 0)
        edge = {-1: (gy < 2) & (row8 >= 6), 1: (gy >= GY - 2) & (row8 < 2)}
        others = {-6: (-2, gx < 4), -2: (0, gx < 2), 3: (0, gx >= GX - 2), 7: (2, gx >= GX - 4)}
        for p in range(low, high):
            x = p - 10
            a = -4 if x < -5 else -2 if x < -1 else 0 if x < 3 else 2 if x < 7 else 4

            def part(b):
                v = s["r3"][slot, 2 + a // 2, 1 + b, x - 2 * a + 2]
                if x in others:
                    near, when = others[x]
                    v = jnp.where(when, s["r3"][slot, 2 + near // 2, 1 + b, x - 2 * near + 2], v)
                return v
            middle = part(0)
            more = pltpu.roll(middle, 80, 1)
            out[p, 0:8, :] = jnp.where(edge[-1], more, part(-1))
            out[p, 8:16, :] = middle
            out[p, 16:24, :] = jnp.where(edge[1], more, part(1))

    def repeat_rows(value, count, rows, start, keep):
        rep = s["rep"]
        for i in range(count):
            v = value[rows * i + start:rows * i + start + keep]
            rep[pl.ds(2 * keep * i, keep, stride=2), :] = v
            rep[pl.ds(2 * keep * i + 1, keep, stride=2), :] = v

    for x in range(16):
        s["k0"][1 + x, 8:40, :] = kap[x]
    to_level1(lambda x: kap[x], s["k1"], 0)
    base1, base2, base3 = 6 * ROUNDS, 6 * ROUNDS + 52, 6 * ROUNDS + 104

    pl.semaphore_wait(barrier, len(PARTNERS))

    moving0 = faces(s["k0"], 0)
    moving1 = send1(s["k1"], 0, base1)
    land(moving0, s["k0"], 0)

    def weights0(x):
        c, others = around0(s["k0"], x, ends(x))
        diag = None
        for i in range(6):
            weight = 0.5 * (c + others[i])
            s["w0"][i, x] = weight
            diag = weight if diag is None else diag + weight
        s["d0"][x] = diag
        inv = OMEGA / diag
        s["i0"][x] = inv
        s["ua"][1 + x, 8:40, :] = rhs[x] * inv
    loop(0, 16, weights0)

    moving0 = faces(s["ua"], 1)
    land1(moving1, s["k1"], 0)
    to_level2(lambda i: s["k1"][1 + i], 0, 8, 0)
    moving2 = send2(0, base2)
    land(moving0, s["ua"], 1)

    def sweep0(src, out):
        def plane(x):
            c, acc = left0(src, x, ends(x))
            out[1 + x, 8:40, :] = c + s["i0"][x] * acc
        loop(0, 16, plane)

    sweep0(s["ua"], s["ub"])
    moving0 = faces(s["ub"], 2)
    land2(moving2, s["k2"], 0)
    to_level3(lambda i: s["k2"][2 + i], 0)
    moving3 = send3(0, base3)
    weights(L1, s["k1"], s["w1"], s["d1"], s["i1"])
    land(moving0, s["ub"], 2)

    def rest0(x):
        residual[x] = left0(s["ub"], x, ends(x))[1]
    loop(0, 16, rest0)
    to_level1(lambda x: residual[x], s["f1"], 1)
    moving1 = send1(s["f1"], 1, base1 + 26)
    weights(L2, s["k2"], s["w2"], s["d2"], s["i2"])
    land3(moving3, s["k3"], 0, 0, 22)
    land1(moving1, s["f1"], 1)

    first(s["u1a"], s["f1"], s["i1"], 1, 17)
    sweep(L1, s["u1a"], s["u1b"], s["f1"], s["w1"], s["d1"], s["i1"], 2, 16)

    def rest1(p):
        s["u1a"][p] = rest(L1, s["u1b"], s["f1"], s["w1"], s["d1"], p)[1]
    loop(3, 15, rest1)
    to_level2(lambda i: s["u1a"][3 + i], 1, 6, 1)
    moving2 = send2(1, base2 + 26)
    weights(L3, s["k3"], s["w3"], s["d3"], s["i3"])
    land2(moving2, s["f2"], 1)

    first(s["u2a"], s["f2"], s["i2"], 1, 15)
    sweep(L2, s["u2a"], s["u2b"], s["f2"], s["w2"], s["d2"], s["i2"], 2, 14)

    def rest2(p):
        s["u2a"][p] = rest(L2, s["u2b"], s["f2"], s["w2"], s["d2"], p)[1]
    s["u2b"][1] = jnp.zeros((24, 128), F32)
    s["u2b"][14] = jnp.zeros((24, 128), F32)
    loop(2, 14, rest2)
    to_level3(lambda i: s["u2a"][2 + i], 1)
    land3(send3(1, base3 + 14), s["f3"], 1, 1, 21)

    u, v = s["u3a"], s["u3b"]
    first(u, s["f3"], s["i3"], 1, 21)
    for step in range(COARSE_SWEEPS - 1):
        sweep(L3, u, v, s["f3"], s["w3"], s["d3"], s["i3"], 2 + step, 20 - step)
        u, v = v, u

    rep = s["rep"]
    value = dot(u[8:14].reshape(6 * 24, 128), repeat_matrix(64))
    repeat_rows(value, 6, 24, 6, 12)
    for p in range(2, 14):
        i = p // 2 - 1
        s["u2b"][p] = s["u2b"][p] + rep[24 * i:24 * i + 24, :]
    sweep(L2, s["u2b"], s["u2a"], s["f2"], s["w2"], s["d2"], s["i2"], 3, 13)
    sweep(L2, s["u2a"], s["u2b"], s["f2"], s["w2"], s["d2"], s["i2"], 4, 12)

    value = dot(s["u2b"][4:12].reshape(8 * 24, 128), repeat_matrix(96))
    repeat_rows(value, 8, 24, 4, 16)
    for p in range(2, 16):
        i = (p + 7) // 2 - 4
        s["u1b"][p] = s["u1b"][p] + rep[32 * i:32 * i + 32, :]
    sweep(L1, s["u1b"], s["u1a"], s["f1"], s["w1"], s["d1"], s["i1"], 3, 15)
    sweep(L1, s["u1a"], s["u1b"], s["f1"], s["w1"], s["d1"], s["i1"], 4, 14)

    value = s["u1b"][4:14].reshape(10 * 32, 128)
    repeat_rows(dot(value, edge_matrix()), 10, 32, 4, 24)
    for x in range(16):
        i = (x + 10) // 2 - 4
        s["h0"][x] = ends(x) + rep[48 * i + 8:48 * i + 40, :]
    repeat_rows(dot(value, repeat_matrix(128)), 10, 32, 4, 24)
    for p in range(18):
        i = (p + 9) // 2 - 4
        if p in (0, 17):
            s["ub"][p, 8:40, :] = s["ub"][p, 8:40, :] + rep[48 * i + 8:48 * i + 40, :]
        else:
            s["ub"][p, 7:41, :] = s["ub"][p, 7:41, :] + rep[48 * i + 7:48 * i + 41, :]

    def up0(x):
        c, acc = left0(s["ub"], x, s["h0"][x])
        s["ua"][1 + x, 8:40, :] = c + s["i0"][x] * acc
    loop(0, 16, up0)
    land(faces(s["ua"], 3), s["ua"], 3)
    sweep0(s["ua"], s["ub"])
    moving0 = faces(s["ub"], 4)
    for x in range(16):
        pressure[x] = s["ub"][1 + x, 8:40, :]
    land(moving0, s["ub"], 4)

    def end0(x):
        residual[x] = left0(s["ub"], x, ends(x))[1]
    loop(0, 16, end0)


def cycle(rhs, kappa):
    block = jax.ShapeDtypeStruct((16, 32, 128), F32)
    vmem = pl.BlockSpec(memory_space=pltpu.VMEM)
    return pl.pallas_call(
        kernel,
        out_shape=(block, block),
        in_specs=[vmem, vmem],
        out_specs=(vmem, vmem),
        scratch_shapes=[pltpu.VMEM(shape, F32) for shape in SCRATCH.values()] + [
            pltpu.SemaphoreType.DMA((COPIES,)), pltpu.SemaphoreType.DMA((COPIES,))],
        compiler_params=pltpu.CompilerParams(
            collective_id=0, has_side_effects=True, vmem_limit_bytes=40 * 1024 * 1024),
        cost_estimate=pl.CostEstimate(flops=40_000_000, bytes_accessed=1_048_576, transcendentals=0),
    )(rhs, kappa)


def solution(mesh):
    placed = (P("gx", "gy", "gz"), P("gx", "gy", "gz"))
    return jax.shard_map(
        cycle, mesh=mesh, in_specs=placed, out_specs=(P("gx", "gy", "gz"), P("gx", "gy", "gz")), check_vma=False)
```

```python
import functools
import itertools

import jax
import jax.numpy as jnp
from jax import lax
from jax.experimental import pallas as pl
from jax.experimental.pallas import tpu as pltpu
from jax.sharding import PartitionSpec as P

MESH = pl.DeviceIdType.MESH
F32 = jnp.float32
OMEGA = 0.8
COARSE_SWEEPS = 8
GX, GY, GZ = 16, 8, 4
FACES = [(-1, 0, 0), (1, 0, 0), (0, -1, 0), (0, 1, 0), (0, 0, -1), (0, 0, 1)]
NEAR = sorted((o for o in itertools.product((-1, 0, 1), repeat=3) if o != (0, 0, 0)), key=lambda o: -sum(map(abs, o)))
FAR = sorted(((a, b, 0) for a in (-4, -2, 0, 2, 4) for b in (-2, 0, 2) if (a, b) != (0, 0)),
             key=lambda o: -sum(map(abs, o)))
ROUNDS = 5

L1 = dict(planes=18, rows=32, px=5, py=8, n=(8, 16, 64), right=72, left=120, level=1)
L2 = dict(planes=16, rows=24, px=6, py=8, n=(4, 8, 32), right=64, left=96, level=2)
L3 = dict(planes=22, rows=24, px=10, py=10, n=(2, 4, 16), right=32, left=112, level=3)

SCRATCH = {
    "ua": (18, 48, 128), "ub": (18, 48, 128), "k0": (18, 48, 128),
    "f0": (16, 32, 128), "w0": (6, 16, 32, 128), "d0": (16, 32, 128), "i0": (16, 32, 128), "h0": (16, 32, 128),
    "ys": (ROUNDS, 2, 16, 128), "zs": (ROUNDS, 8, 128),
    "rx": (ROUNDS, 2, 32, 128), "ry": (ROUNDS, 2, 16, 128), "rz": (ROUNDS, 2, 8, 128), "mz": (8, 128),
    "sum": (256, 128), "rep": (10 * 48, 128),
    "k1": (18, 32, 128), "f1": (18, 32, 128), "u1a": (18, 32, 128), "u1b": (18, 32, 128),
    "w1": (6, 18, 32, 128), "d1": (18, 32, 128), "i1": (18, 32, 128),
    "zp1": (2, 16, 128), "zb1": (2, 2, 3, 32, 128),
    "k2": (16, 24, 128), "f2": (16, 24, 128), "u2a": (16, 24, 128), "u2b": (16, 24, 128),
    "w2": (6, 16, 24, 128), "d2": (16, 24, 128), "i2": (16, 24, 128),
    "p2": (2, 2, 8, 128), "r2": (2, 27, 2, 8, 128),
    "k3": (22, 24, 128), "f3": (22, 24, 128), "u3a": (22, 24, 128), "u3b": (22, 24, 128),
    "w3": (6, 22, 24, 128), "d3": (22, 24, 128), "i3": (22, 24, 128),
    "s3": (2, 6, 8, 128), "r3": (2, 5, 3, 6, 8, 128),
}
COPIES = ROUNDS * 6 + 2 * (26 + 26 + 14)


def lanes(shape):
    return lax.broadcasted_iota(jnp.int32, shape, len(shape) - 1)


def loop(low, high, body):
    def step(i, carry):
        body(i)
        return carry
    lax.fori_loop(low, high, step, 0, unroll=True)


def dot(a, b):
    return jnp.dot(a, b, precision=lax.Precision.HIGHEST, preferred_element_type=F32)


def pool_matrix(split):
    row = lax.broadcasted_iota(jnp.int32, (128, 128), 0)
    col = lax.broadcasted_iota(jnp.int32, (128, 128), 1)
    target = jnp.where(row < split, row // 2, 64 + row // 2)
    return jnp.where(target == col, 0.125, 0.0).astype(F32)


def repeat_matrix(split):
    row = lax.broadcasted_iota(jnp.int32, (128, 128), 0)
    col = lax.broadcasted_iota(jnp.int32, (128, 128), 1)
    origin = jnp.where(col < split, col // 2, 64 + col // 2)
    return jnp.where(origin == row, 1.0, 0.0).astype(F32)


def edge_matrix():
    row = lax.broadcasted_iota(jnp.int32, (128, 128), 0)
    col = lax.broadcasted_iota(jnp.int32, (128, 128), 1)
    hit = ((row == 127) & (col == 0)) | ((row == 64) & (col == 127))
    return jnp.where(hit, 1.0, 0.0).astype(F32)


def kernel(rhs_in, kap_in, pressure, residual, *refs):
    s = dict(zip(SCRATCH, refs))
    send, recv, load = refs[len(SCRATCH):]
    rhs = s["f0"]
    gx, gy, gz = lax.axis_index("gx"), lax.axis_index("gy"), lax.axis_index("gz")

    def device(o):
        return (lax.rem(gx + (o[0] + GX), GX), lax.rem(gy + (o[1] + GY), GY), lax.rem(gz + (o[2] + GZ), GZ))

    def copy(src, dst, o, index):
        return pltpu.make_async_remote_copy(
            src_ref=src, dst_ref=dst, send_sem=send.at[index], recv_sem=recv.at[index],
            device_id=device(o), device_id_type=MESH)

    barrier = pltpu.get_barrier_semaphore()
    for o in FACES:
        pl.semaphore_signal(barrier, inc=1, device_id=device(o), device_id_type=MESH)
    load_kap = pltpu.make_async_copy(kap_in, s["k0"].at[pl.ds(1, 16), pl.ds(8, 32)], load.at[0])
    load_rhs = pltpu.make_async_copy(rhs_in, rhs, load.at[1])
    load_kap.start()
    load_rhs.start()

    lane8 = lanes((8, 128))
    lane32 = lanes((32, 128))
    total = s["sum"]

    def faces(u, r):
        for x in range(16):
            s["ys"][r, 0, x:x + 1, :] = u[1 + x, 8:9, :]
            s["ys"][r, 1, x:x + 1, :] = u[1 + x, 39:40, :]
        packed = jnp.zeros((8, 128), F32)
        for x in range(16):
            for t in range(4):
                k = 4 * x + t
                moved = pltpu.roll(u[1 + x, 8 + 8 * t:16 + 8 * t, :], (2 * k + 1) % 128, 1)
                packed = jnp.where((lane8 >> 1) == k, moved, packed)
        s["zs"][r] = packed
        base = 6 * r
        copies = []
        for i, o in enumerate(FACES):
            low = i % 2 == 0
            side = 1 if low else 0
            if i < 2:
                src, dst = u.at[1 if low else 16, pl.ds(8, 32)], s["rx"].at[r, side]
            elif i < 4:
                src, dst = s["ys"].at[r, 0 if low else 1], s["ry"].at[r, side]
            else:
                src, dst = s["zs"].at[r], s["rz"].at[r, side]
            copies.append(copy(src, dst, o, base + i))
        for c in copies:
            c.start()
        return copies

    def land(copies, u, r):
        for c in copies:
            c.wait()
        u[0, 8:40, :] = jnp.where(gx > 0, s["rx"][r, 0], 0.0)
        u[17, 8:40, :] = jnp.where(gx < GX - 1, s["rx"][r, 1], 0.0)
        below = jnp.where(gy > 0, s["ry"][r, 0], 0.0)
        above = jnp.where(gy < GY - 1, s["ry"][r, 1], 0.0)
        for x in range(16):
            u[1 + x, 7:8, :] = below[x:x + 1]
            u[1 + x, 40:41, :] = above[x:x + 1]
        left = jnp.where(gz > 0, s["rz"][r, 0], 0.0)
        right = jnp.where(gz < GZ - 1, s["rz"][r, 1], 0.0)
        s["mz"][...] = jnp.where((lane8 & 1) == 0, left, pltpu.roll(right, 126, 1))

    def ends(x):
        packed = s["mz"][...]
        return jnp.concatenate(
            [pltpu.roll(packed, lax.rem(256 - 8 * x - 2 * t, 128), 1) for t in range(4)], axis=0)

    def around0(u, x, end):
        c = u[1 + x, 8:40, :]
        return c, [
            u[x, 8:40, :], u[2 + x, 8:40, :], u[1 + x, 7:39, :], u[1 + x, 9:41, :],
            jnp.where(lane32 == 0, end, pltpu.roll(c, 1, 1)),
            jnp.where(lane32 == 127, end, pltpu.roll(c, 127, 1))]

    def left0(u, x, end):
        c, others = around0(u, x, end)
        acc = rhs[x] - s["d0"][x] * c
        for i in range(6):
            acc = acc + s["w0"][i, x] * others[i]
        return c, acc

    def inside(lv, p):
        n, level = lv["n"], lv["level"]
        shape = (lv["rows"], 128)
        lane = lanes(shape)
        row = lax.broadcasted_iota(jnp.int32, shape, 0)
        x = gx * n[0] + (p - lv["px"])
        y = gy * n[1] + (row - lv["py"])
        z = gz * n[2] + jnp.where(lane < lv["right"], lane, lane - 128)
        ok = (lane < lv["right"]) | (lane >= lv["left"])
        ok = ok & (y >= 0) & (y < 256 >> level) & (z >= 0) & (z < 512 >> level)
        return ok & (x >= 0) & (x < 256 >> level)

    def around(u, p, rows):
        c = u[p]
        return c, [u[p - 1], u[p + 1], pltpu.roll(c, 1, 0), pltpu.roll(c, rows - 1, 0),
                   pltpu.roll(c, 1, 1), pltpu.roll(c, 127, 1)]

    def weights(lv, k, w, d, inv):
        scale = 0.5 * 0.25 ** lv["level"]

        def clear(p):
            k[p] = jnp.where(inside(lv, p), k[p], 0.0)

        row = lax.broadcasted_iota(jnp.int32, (lv["rows"], 128), 0)
        ends_y = {2: row == 0, 3: row == lv["rows"] - 1}

        def plane(p):
            c, others = around(k, p, lv["rows"])
            diag = None
            for i in range(6):
                other = jnp.where(ends_y[i], 0.0, others[i]) if i in ends_y else others[i]
                weight = scale * (c + other)
                w[i, p] = jnp.where(ends_y[i], 0.0, weight) if i in ends_y else weight
                diag = weight if diag is None else diag + weight
            d[p] = diag
            inv[p] = jnp.where(inside(lv, p), OMEGA / diag, 0.0)
        loop(0, lv["planes"], clear)
        loop(1, lv["planes"] - 1, plane)

    def rest(lv, u, f, w, d, p):
        c, others = around(u, p, lv["rows"])
        acc = f[p] - d[p] * c
        for i in range(6):
            acc = acc + w[i, p] * others[i]
        return c, acc

    def sweep(lv, u, v, f, w, d, inv, low, high):
        def plane(p):
            c, acc = rest(lv, u, f, w, d, p)
            v[p] = c + inv[p] * acc
        loop(low, high, plane)

    def first(u, f, inv, low, high):
        def plane(p):
            u[p] = f[p] * inv[p]
        loop(low, high, plane)

    def pooled_rows(count, rows, start, keep):
        parts = []
        for i in range(count):
            parts.append(total[pl.ds(rows * i + start, keep, stride=2), :]
                         + total[pl.ds(rows * i + start + 1, keep, stride=2), :])
        return jnp.concatenate(parts, axis=0)

    def sums(count, rows, plane):
        for i in range(count):
            total[rows * i:rows * i + rows, :] = plane(2 * i) + plane(2 * i + 1)

    def to_level1(plane, out, slot):
        sums(8, 32, plane)
        mean = dot(pooled_rows(8, 32, 0, 16), pool_matrix(128))
        for i in range(8):
            out[5 + i, 8:24, :] = mean[16 * i:16 * i + 16]
        lane16 = lanes((16, 128))
        packed = jnp.zeros((16, 128), F32)
        for i in range(8):
            v = mean[16 * i:16 * i + 16]
            packed = jnp.where((lane16 >= 16 * i) & (lane16 < 16 * i + 8), pltpu.roll(v, 16 * i, 1) if i else v, packed)
            packed = jnp.where((lane16 >= 16 * i + 8) & (lane16 < 16 * i + 16),
                               pltpu.roll(v, (16 * i + 8 - 56) % 128, 1), packed)
        s["zp1"][slot] = packed

    def send1(out, slot, base):
        copies = []
        for i, (a, b, c) in enumerate(NEAR):
            rows_src = {-1: (8, 8), 0: (8, 16), 1: (16, 8)}[b]
            rows_dst = {-1: 24, 0: 8, 1: 0}[b]
            if c == 0:
                first_plane, count, to = {-1: (5, 5, 13), 0: (5, 8, 5), 1: (8, 5, 0)}[a]
                src = out.at[pl.ds(first_plane, count), pl.ds(rows_src[0], rows_src[1])]
                dst = out.at[pl.ds(to, count), pl.ds(rows_dst, rows_src[1])]
            else:
                src = s["zp1"].at[slot, pl.ds(rows_src[0] - 8, rows_src[1])]
                dst = s["zb1"].at[slot, 0 if c == 1 else 1, 1 - a, pl.ds(rows_dst, rows_src[1])]
            copies.append(copy(src, dst, (a, b, c), base + i))
        for c in copies:
            c.start()
        return copies

    def land1(copies, out, slot):
        for c in copies:
            c.wait()
        for p in range(18):
            x = p - 5
            a = -1 if x < 0 else (0 if x < 8 else 1)
            q = x - 8 * a
            low = pltpu.roll(s["zb1"][slot, 0, a + 1], (120 - 16 * q - 8) % 128, 1)
            high = pltpu.roll(s["zb1"][slot, 1, a + 1], (64 - 16 * q) % 128, 1)
            out[p] = jnp.where(lane32 < 64, out[p],
                               jnp.where(lane32 < 72, high, jnp.where(lane32 >= 120, low, 0.0)))

    def to_level2(plane, first_q, count, slot):
        sums(count, 32, plane)
        rows = pooled_rows(count, 32, 8, 8)
        rows = jnp.where(lanes(rows.shape) < 64, rows, 0.0)
        mean = dot(rows, pool_matrix(128))
        packs = [jnp.zeros((8, 128), F32), jnp.zeros((8, 128), F32)]
        for i in range(count):
            q = first_q + i
            v = mean[8 * i:8 * i + 8]
            packs[q // 4] = packs[q // 4] + (pltpu.roll(v, 32 * (q % 4), 1) if q % 4 else v)
        s["p2"][slot, 0] = packs[0]
        s["p2"][slot, 1] = packs[1]

    def slot2(a, b, c):
        return 9 * (a + 1) + 3 * (b + 1) + (c + 1)

    def send2(slot, base):
        copies = []
        for i, o in enumerate(NEAR):
            copies.append(copy(s["p2"].at[slot], s["r2"].at[slot, slot2(-o[0], -o[1], -o[2])], o, base + i))
        for c in copies:
            c.start()
        s["r2"][slot, slot2(0, 0, 0)] = s["p2"][slot]
        return copies

    def land2(copies, out, slot):
        for c in copies:
            c.wait()
        for p in range(16):
            x = p - 6
            a = -1 if x < 0 else (0 if x < 4 else 1)
            q = x - 4 * a + 2

            def part(b, c, place):
                v = s["r2"][slot, slot2(a, b, c), q // 4]
                shift = (place - 32 * (q % 4)) % 128
                return pltpu.roll(v, shift, 1) if shift else v
            for b in (-1, 0, 1):
                out[p, 8 * (b + 1):8 * (b + 2), :] = jnp.where(
                    lane8 < 32, part(b, 0, 0),
                    jnp.where(lane8 < 64, part(b, 1, 32), jnp.where(lane8 >= 96, part(b, -1, 96), 0.0)))

    def to_level3(plane, slot):
        for i in range(6):
            v = plane(2 * i) + plane(2 * i + 1)
            total[40 * i:40 * i + 24, :] = v
            total[40 * i + 24:40 * i + 32, :] = v[:8]
            total[40 * i + 32:40 * i + 40, :] = v[:8]
        rows = jnp.concatenate([pooled_rows(6, 40, 4, 8), pooled_rows(6, 40, 20, 8)], axis=0)
        mean = dot(rows, pool_matrix(64))
        for i in range(6):
            more = pltpu.roll(mean[48 + 8 * i:56 + 8 * i], 48, 1)
            s["s3"][slot, i] = jnp.where((lane8 >= 32) & (lane8 < 80), more, mean[8 * i:8 * i + 8])

    def send3(slot, base):
        copies = []
        for i, (a, b, c) in enumerate(FAR):
            start, count = {0: (0, 6), 2: (0, 5), -2: (1, 5), 4: (0, 5), -4: (1, 5)}[a]
            if slot == 1 and abs(a) == 4:
                start, count = 1, 4
            copies.append(copy(
                s["s3"].at[slot, pl.ds(start, count)],
                s["r3"].at[slot, 2 - a // 2, 1 - b // 2, pl.ds(start, count)], (a, b, c), base + i))
        for c in copies:
            c.start()
        s["r3"][slot, 2, 1] = s["s3"][slot]
        return copies

    def land3(copies, out, slot, low, high):
        for c in copies:
            c.wait()
        row8 = lax.broadcasted_iota(jnp.int32, (8, 128), 0)
        edge = {-1: (gy < 2) & (row8 >= 6), 1: (gy >= GY - 2) & (row8 < 2)}
        others = {-6: (-2, gx < 4), -2: (0, gx < 2), 3: (0, gx >= GX - 2), 7: (2, gx >= GX - 4)}
        for p in range(low, high):
            x = p - 10
            a = -4 if x < -5 else -2 if x < -1 else 0 if x < 3 else 2 if x < 7 else 4

            def part(b):
                v = s["r3"][slot, 2 + a // 2, 1 + b, x - 2 * a + 2]
                if x in others:
                    near, when = others[x]
                    v = jnp.where(when, s["r3"][slot, 2 + near // 2, 1 + b, x - 2 * near + 2], v)
                return v
            middle = part(0)
            more = pltpu.roll(middle, 80, 1)
            out[p, 0:8, :] = jnp.where(edge[-1], more, part(-1))
            out[p, 8:16, :] = middle
            out[p, 16:24, :] = jnp.where(edge[1], more, part(1))

    def repeat_rows(value, count, rows, start, keep):
        rep = s["rep"]
        for i in range(count):
            v = value[rows * i + start:rows * i + start + keep]
            rep[pl.ds(2 * keep * i, keep, stride=2), :] = v
            rep[pl.ds(2 * keep * i + 1, keep, stride=2), :] = v

    base1, base2, base3 = 6 * ROUNDS, 6 * ROUNDS + 52, 6 * ROUNDS + 104
    load_kap.wait()
    pl.semaphore_wait(barrier, len(FACES))
    moving0 = faces(s["k0"], 0)
    to_level1(lambda x: s["k0"][1 + x, 8:40, :], s["k1"], 0)
    load_rhs.wait()
    land(moving0, s["k0"], 0)

    def weights0(x):
        c, others = around0(s["k0"], x, ends(x))
        diag = None
        for i in range(6):
            weight = 0.5 * (c + others[i])
            s["w0"][i, x] = weight
            diag = weight if diag is None else diag + weight
        s["d0"][x] = diag
        inv = OMEGA / diag
        s["i0"][x] = inv
        s["ua"][1 + x, 8:40, :] = rhs[x] * inv
    loop(0, 16, weights0)

    moving0 = faces(s["ua"], 1)
    land(moving0, s["ua"], 1)

    def sweep0(src, out):
        def plane(x):
            c, acc = left0(src, x, ends(x))
            out[1 + x, 8:40, :] = c + s["i0"][x] * acc
        loop(0, 16, plane)

    sweep0(s["ua"], s["ub"])
    moving0 = faces(s["ub"], 2)
    coefficient1 = send1(s["k1"], 0, base1)
    land(moving0, s["ub"], 2)

    def rest0(x):
        residual[x] = left0(s["ub"], x, ends(x))[1]
    loop(0, 16, rest0)
    to_level1(lambda x: residual[x], s["f1"], 1)
    moving1 = send1(s["f1"], 1, base1 + 26)
    land1(coefficient1, s["k1"], 0)
    to_level2(lambda i: s["k1"][1 + i], 0, 8, 0)
    coefficient2 = send2(0, base2)
    weights(L1, s["k1"], s["w1"], s["d1"], s["i1"])
    land1(moving1, s["f1"], 1)

    first(s["u1a"], s["f1"], s["i1"], 1, 17)
    sweep(L1, s["u1a"], s["u1b"], s["f1"], s["w1"], s["d1"], s["i1"], 2, 16)

    def rest1(p):
        s["u1a"][p] = rest(L1, s["u1b"], s["f1"], s["w1"], s["d1"], p)[1]
    loop(3, 15, rest1)
    to_level2(lambda i: s["u1a"][3 + i], 1, 6, 1)
    moving2 = send2(1, base2 + 26)
    land2(coefficient2, s["k2"], 0)
    to_level3(lambda i: s["k2"][2 + i], 0)
    coefficient3 = send3(0, base3)
    weights(L2, s["k2"], s["w2"], s["d2"], s["i2"])
    land2(moving2, s["f2"], 1)

    first(s["u2a"], s["f2"], s["i2"], 1, 15)
    sweep(L2, s["u2a"], s["u2b"], s["f2"], s["w2"], s["d2"], s["i2"], 2, 14)

    def rest2(p):
        s["u2a"][p] = rest(L2, s["u2b"], s["f2"], s["w2"], s["d2"], p)[1]
    s["u2b"][1] = jnp.zeros((24, 128), F32)
    s["u2b"][14] = jnp.zeros((24, 128), F32)
    loop(2, 14, rest2)
    to_level3(lambda i: s["u2a"][2 + i], 1)
    moving3 = send3(1, base3 + 14)
    land3(coefficient3, s["k3"], 0, 0, 22)
    weights(L3, s["k3"], s["w3"], s["d3"], s["i3"])
    land3(moving3, s["f3"], 1, 1, 21)

    u, v = s["u3a"], s["u3b"]
    first(u, s["f3"], s["i3"], 1, 21)
    for step in range(COARSE_SWEEPS - 1):
        sweep(L3, u, v, s["f3"], s["w3"], s["d3"], s["i3"], 2 + step, 20 - step)
        u, v = v, u

    rep = s["rep"]
    value = dot(u[8:14].reshape(6 * 24, 128), repeat_matrix(64))
    repeat_rows(value, 6, 24, 6, 12)
    for p in range(2, 14):
        i = p // 2 - 1
        s["u2b"][p] = s["u2b"][p] + rep[24 * i:24 * i + 24, :]
    sweep(L2, s["u2b"], s["u2a"], s["f2"], s["w2"], s["d2"], s["i2"], 3, 13)
    sweep(L2, s["u2a"], s["u2b"], s["f2"], s["w2"], s["d2"], s["i2"], 4, 12)

    value = dot(s["u2b"][4:12].reshape(8 * 24, 128), repeat_matrix(96))
    repeat_rows(value, 8, 24, 4, 16)
    for p in range(2, 16):
        i = (p + 7) // 2 - 4
        s["u1b"][p] = s["u1b"][p] + rep[32 * i:32 * i + 32, :]
    sweep(L1, s["u1b"], s["u1a"], s["f1"], s["w1"], s["d1"], s["i1"], 3, 15)
    sweep(L1, s["u1a"], s["u1b"], s["f1"], s["w1"], s["d1"], s["i1"], 4, 14)

    value = s["u1b"][4:14].reshape(10 * 32, 128)
    repeat_rows(dot(value, edge_matrix()), 10, 32, 4, 24)
    for x in range(16):
        i = (x + 10) // 2 - 4
        s["h0"][x] = ends(x) + rep[48 * i + 8:48 * i + 40, :]
    repeat_rows(dot(value, repeat_matrix(128)), 10, 32, 4, 24)
    for p in range(18):
        i = (p + 9) // 2 - 4
        if p in (0, 17):
            s["ub"][p, 8:40, :] = s["ub"][p, 8:40, :] + rep[48 * i + 8:48 * i + 40, :]
        else:
            s["ub"][p, 7:41, :] = s["ub"][p, 7:41, :] + rep[48 * i + 7:48 * i + 41, :]

    def up0(x):
        c, acc = left0(s["ub"], x, s["h0"][x])
        s["ua"][1 + x, 8:40, :] = c + s["i0"][x] * acc
    loop(0, 16, up0)
    land(faces(s["ua"], 3), s["ua"], 3)
    sweep0(s["ua"], s["ub"])
    moving0 = faces(s["ub"], 4)
    for x in range(16):
        pressure[x] = s["ub"][1 + x, 8:40, :]
    land(moving0, s["ub"], 4)

    def end0(x):
        residual[x] = left0(s["ub"], x, ends(x))[1]
    loop(0, 16, end0)


def cycle(rhs, kappa):
    block = jax.ShapeDtypeStruct((16, 32, 128), F32)
    vmem = pl.BlockSpec(memory_space=pltpu.VMEM)
    return pl.pallas_call(
        kernel,
        out_shape=(block, block),
        in_specs=[pl.BlockSpec(memory_space=pltpu.HBM)] * 2,
        out_specs=(vmem, vmem),
        scratch_shapes=[pltpu.VMEM(shape, F32) for shape in SCRATCH.values()] + [
            pltpu.SemaphoreType.DMA((COPIES,)), pltpu.SemaphoreType.DMA((COPIES,)),
            pltpu.SemaphoreType.DMA((2,))],
        compiler_params=pltpu.CompilerParams(
            collective_id=0, has_side_effects=True, vmem_limit_bytes=40 * 1024 * 1024),
        cost_estimate=pl.CostEstimate(flops=40_000_000, bytes_accessed=1_048_576, transcendentals=0),
    )(rhs, kappa)


def solution(mesh):
    placed = (P("gx", "gy", "gz"), P("gx", "gy", "gz"))
    return jax.shard_map(
        cycle, mesh=mesh, in_specs=placed, out_specs=(P("gx", "gy", "gz"), P("gx", "gy", "gz")), check_vma=False)
```

```python
import functools
import itertools

import jax
import jax.numpy as jnp
from jax import lax
from jax.experimental import pallas as pl
from jax.experimental.pallas import tpu as pltpu
from jax.sharding import PartitionSpec as P

MESH = pl.DeviceIdType.MESH
F32 = jnp.float32
BF16 = jnp.bfloat16
OMEGA = 0.8
COARSE_SWEEPS = 8
GX, GY, GZ = 16, 8, 4
FACES = [(-1, 0, 0), (1, 0, 0), (0, -1, 0), (0, 1, 0), (0, 0, -1), (0, 0, 1)]
NEAR = sorted((o for o in itertools.product((-1, 0, 1), repeat=3) if o != (0, 0, 0)), key=lambda o: -sum(map(abs, o)))
FAR = sorted(((a, b, 0) for a in (-4, -2, 0, 2, 4) for b in (-2, 0, 2) if (a, b) != (0, 0)),
             key=lambda o: -sum(map(abs, o)))
ROUNDS = 5
PAIRS = [(0, 5), (1, 2), (3, 4)]

L1 = dict(planes=18, rows=32, px=5, py=8, n=(8, 16, 64), right=72, left=120, level=1)
L2 = dict(planes=16, rows=24, px=6, py=8, n=(4, 8, 32), right=64, left=96, level=2)
L3 = dict(planes=22, rows=24, px=10, py=10, n=(2, 4, 16), right=32, left=112, level=3)

SCRATCH = {
    "ua": (18, 48, 128), "ub": (18, 48, 128), "k0": (18, 48, 128),
    "f0": (16, 32, 128), "part": (16, 32, 128), "wy": (16, 32, 128), "wz": (16, 32, 128), "w0": (6, 16, 32, 128), "d0": (16, 32, 128), "i0": (16, 32, 128), "h0": (16, 32, 128),
    "ys": (ROUNDS, 2, 16, 128), "zs": (ROUNDS, 8, 128),
    "rx": (ROUNDS, 2, 32, 128), "ry": (ROUNDS, 2, 16, 128), "rz": (ROUNDS, 2, 8, 128), "mz": (2, 8, 128),
    "sum": (256, 128), "rep": (10 * 48, 128),
    "k1": (18, 32, 128), "f1": (18, 32, 128), "u1a": (18, 32, 128), "u1b": (18, 32, 128),
    "w1": (6, 18, 32, 128), "d1": (18, 32, 128), "i1": (18, 32, 128),
    "zp1": (2, 16, 128), "zb1": (2, 2, 3, 32, 128),
    "k2": (16, 24, 128), "f2": (16, 24, 128), "u2a": (16, 24, 128), "u2b": (16, 24, 128),
    "w2": (6, 16, 24, 128), "d2": (16, 24, 128), "i2": (16, 24, 128),
    "p2": (2, 2, 8, 128), "r2": (2, 27, 2, 8, 128),
    "k3": (22, 24, 128), "f3": (22, 24, 128), "u3a": (22, 24, 128), "u3b": (22, 24, 128),
    "w3": (6, 22, 24, 128), "d3": (22, 24, 128), "i3": (22, 24, 128),
    "s3": (2, 6, 8, 128), "t3": (2, 3, 8, 128), "r3": (2, 5, 6, 8, 128), "q3": (2, 5, 2, 3, 8, 128),
}
COPIES = ROUNDS * 6 + 2 * (26 + 26 + 14)


def lanes(shape):
    return lax.broadcasted_iota(jnp.int32, shape, len(shape) - 1)


def loop(low, high, body):
    def step(i, carry):
        body(i)
        return carry
    lax.fori_loop(low, high, step, 0, unroll=True)


def dot(a, b):
    high = a.astype(BF16)
    low = (a - high.astype(F32)).astype(BF16)
    return (jnp.dot(high, b, preferred_element_type=F32) + jnp.dot(low, b, preferred_element_type=F32))


def tables():
    row = lax.broadcasted_iota(jnp.int32, (128, 128), 0)
    col = lax.broadcasted_iota(jnp.int32, (128, 128), 1)

    def half(index, split):
        return jnp.where(index < split, index // 2, 64 + index // 2)
    pools = [jnp.where(half(row, split) == col, 0.125, 0.0) for split in (128, 64)]
    repeats = [jnp.where(half(col, split) == row, 1.0, 0.0) for split in (64, 96, 128)]
    edges = jnp.where(((row == 127) & (col == 0)) | ((row == 64) & (col == 127)), 1.0, 0.0)
    return [m.astype(BF16) for m in pools + repeats + [edges]]


POOL, POOL_HALO, REPEAT_64, REPEAT_96, REPEAT_128, EDGES = range(6)


def kernel(rhs_in, kap_in, pressure, residual, *refs):
    s = dict(zip(SCRATCH, refs))
    send, recv, load, tab = refs[len(SCRATCH):]
    rhs = s["f0"]
    gx, gy, gz = lax.axis_index("gx"), lax.axis_index("gy"), lax.axis_index("gz")

    at_x = {a: (gx + a) & (GX - 1) for a in (-4, -2, -1, 1, 2, 4)} | {0: gx}
    at_y = {a: (gy + a) & (GY - 1) for a in (-2, -1, 1, 2)} | {0: gy}
    at_z = {a: (gz + a) & (GZ - 1) for a in (-1, 1)} | {0: gz}
    sent = []

    def device(o):
        return (at_x[o[0]], at_y[o[1]], at_z[o[2]])

    def drain():
        for c in sent:
            c.wait_send()
        sent.clear()

    def copy(src, dst, o, index):
        return pltpu.make_async_remote_copy(
            src_ref=src, dst_ref=dst, send_sem=send.at[index], recv_sem=recv.at[index],
            device_id=device(o), device_id_type=MESH)

    barrier = pltpu.get_barrier_semaphore()
    for o in FACES:
        pl.semaphore_signal(barrier, inc=1, device_id=device(o), device_id_type=MESH)
    load_kap = pltpu.make_async_copy(kap_in, s["k0"].at[pl.ds(1, 16), pl.ds(8, 32)], load.at[0])
    load_rhs = pltpu.make_async_copy(rhs_in, rhs, load.at[1])
    load_kap.start()
    load_rhs.start()

    lane8 = lanes((8, 128))
    lane32 = lanes((32, 128))
    total = s["sum"]

    def pack(u, r):
        for x in range(16):
            s["ys"][r, 0, x:x + 1, :] = u[1 + x, 8:9, :]
            s["ys"][r, 1, x:x + 1, :] = u[1 + x, 39:40, :]
        packed = jnp.zeros((8, 128), F32)
        for x in range(16):
            for t in range(4):
                k = 4 * x + t
                moved = pltpu.roll(u[1 + x, 8 + 8 * t:16 + 8 * t, :], (2 * k + 1) % 128, 1)
                packed = jnp.where((lane8 >> 1) == k, moved, packed)
        s["zs"][r] = packed

    def faces(u, r):
        base = 6 * r
        copies = []
        for i, o in enumerate(FACES):
            low = i % 2 == 0
            side = 1 if low else 0
            if i < 2:
                src, dst = u.at[1 if low else 16, pl.ds(8, 32)], s["rx"].at[r, side]
            elif i < 4:
                src, dst = s["ys"].at[r, 0 if low else 1], s["ry"].at[r, side]
            else:
                src, dst = s["zs"].at[r], s["rz"].at[r, side]
            copies.append(copy(src, dst, o, base + i))
        for c in copies:
            c.start()
        drain()
        return copies

    def arrive(copies):
        for c in copies:
            c.wait_recv()
        sent.extend(copies)

    def land(u, r, out):
        u[0, 8:40, :] = jnp.where(gx > 0, s["rx"][r, 0], 0.0)
        u[17, 8:40, :] = jnp.where(gx < GX - 1, s["rx"][r, 1], 0.0)
        below = jnp.where(gy > 0, s["ry"][r, 0], 0.0)
        above = jnp.where(gy < GY - 1, s["ry"][r, 1], 0.0)
        for x in range(16):
            u[1 + x, 7:8, :] = below[x:x + 1]
            u[1 + x, 40:41, :] = above[x:x + 1]
        merge(r, out)

    def merge(r, out):
        left = jnp.where(gz > 0, s["rz"][r, 0], 0.0)
        right = jnp.where(gz < GZ - 1, s["rz"][r, 1], 0.0)
        s["mz"][out] = jnp.where((lane8 & 1) == 0, left, pltpu.roll(right, 126, 1))

    def ends(x, at):
        packed = s["mz"][at]
        return jnp.concatenate(
            [pltpu.roll(packed, (-8 * x - 2 * t) % 128, 1) if x + t else packed for t in range(4)], axis=0)

    def around0(u, x):
        c = u[1 + x, 8:40, :]
        return c, [u[x, 8:40, :], u[2 + x, 8:40, :], u[1 + x, 7:39, :], u[1 + x, 9:41, :],
                   pltpu.roll(c, 1, 1), pltpu.roll(c, 127, 1)]

    def core0(u, x):
        c, others = around0(u, x)
        acc = rhs[x] - s["d0"][x] * c
        for i in range(6):
            acc = acc + s["w0"][i, x] * others[i]
        return c, acc

    def partial0(u):
        for x in range(16):
            s["part"][x] = core0(u, x)[1]

    def finish0(r, x):
        acc = s["part"][x] + s["wz"][x] * ends(x, 0)
        if x == 0:
            acc = acc + s["w0"][0, 0] * jnp.where(gx > 0, s["rx"][r, 0], 0.0)
        if x == 15:
            acc = acc + s["w0"][1, 15] * jnp.where(gx < GX - 1, s["rx"][r, 1], 0.0)
        below = jnp.broadcast_to(jnp.where(gy > 0, s["ry"][r, 0, x:x + 1, :], 0.0), (8, 128))
        above = jnp.broadcast_to(jnp.where(gy < GY - 1, s["ry"][r, 1, x:x + 1, :], 0.0), (8, 128))
        return jnp.concatenate(
            [acc[:8] + s["wy"][x, :8] * below, acc[8:24], acc[24:] + s["wy"][x, 24:] * above], axis=0)

    def clear0(u):
        u[0] = jnp.zeros((48, 128), F32)
        u[17] = jnp.zeros((48, 128), F32)
        for x in range(16):
            u[1 + x, 0:8, :] = jnp.zeros((8, 128), F32)
            u[1 + x, 40:48, :] = jnp.zeros((8, 128), F32)

    def inside(lv, p):
        n, level = lv["n"], lv["level"]
        shape = (lv["rows"], 128)
        lane = lanes(shape)
        row = lax.broadcasted_iota(jnp.int32, shape, 0)
        x = gx * n[0] + (p - lv["px"])
        y = gy * n[1] + (row - lv["py"])
        z = gz * n[2] + jnp.where(lane < lv["right"], lane, lane - 128)
        ok = (lane < lv["right"]) | (lane >= lv["left"])
        ok = ok & (y >= 0) & (y < 256 >> level) & (z >= 0) & (z < 512 >> level)
        return ok & (x >= 0) & (x < 256 >> level)

    def around(u, p, rows):
        c = u[p]
        return c, [u[p - 1], u[p + 1], pltpu.roll(c, 1, 0), pltpu.roll(c, rows - 1, 0),
                   pltpu.roll(c, 1, 1), pltpu.roll(c, 127, 1)]

    def weights(lv, k, w, d, inv):
        scale = 0.5 * 0.25 ** lv["level"]

        def clear(p):
            k[p] = jnp.where(inside(lv, p), k[p], 0.0)

        row = lax.broadcasted_iota(jnp.int32, (lv["rows"], 128), 0)
        ends_y = {2: row == 0, 3: row == lv["rows"] - 1}

        def plane(p):
            c, others = around(k, p, lv["rows"])
            diag = None
            for i in range(6):
                other = jnp.where(ends_y[i], 0.0, others[i]) if i in ends_y else others[i]
                weight = scale * (c + other)
                w[i, p] = jnp.where(ends_y[i], 0.0, weight) if i in ends_y else weight
                diag = weight if diag is None else diag + weight
            d[p] = diag
            inv[p] = jnp.where(inside(lv, p), OMEGA / diag, 0.0)
        loop(0, lv["planes"], clear)
        loop(1, lv["planes"] - 1, plane)

    def rest(lv, u, f, w, d, p):
        c, others = around(u, p, lv["rows"])
        acc = f[p] - d[p] * c
        for i in range(6):
            acc = acc + w[i, p] * others[i]
        return c, acc

    def sweep(lv, u, v, f, w, d, inv, low, high):
        def plane(p):
            c, others = around(u, p, lv["rows"])
            acc = f[p]
            for i in range(6):
                acc = acc + w[i, p] * others[i]
            v[p] = (1.0 - OMEGA) * c + inv[p] * acc
        loop(low, high, plane)

    def first(u, f, inv, low, high):
        def plane(p):
            u[p] = f[p] * inv[p]
        loop(low, high, plane)

    def pooled_rows(count, rows, start, keep):
        parts = []
        for i in range(count):
            parts.append(total[pl.ds(rows * i + start, keep, stride=2), :]
                         + total[pl.ds(rows * i + start + 1, keep, stride=2), :])
        return jnp.concatenate(parts, axis=0)

    def sums(count, rows, plane):
        for i in range(count):
            total[rows * i:rows * i + rows, :] = plane(2 * i) + plane(2 * i + 1)

    def to_level1(plane, out, slot):
        sums(8, 32, plane)
        mean = dot(pooled_rows(8, 32, 0, 16), tab[POOL])
        for i in range(8):
            out[5 + i, 8:24, :] = mean[16 * i:16 * i + 16]
        lane16 = lanes((16, 128))
        packed = jnp.zeros((16, 128), F32)
        for i in range(8):
            v = mean[16 * i:16 * i + 16]
            packed = jnp.where((lane16 >= 16 * i) & (lane16 < 16 * i + 8), pltpu.roll(v, 16 * i, 1) if i else v, packed)
            packed = jnp.where((lane16 >= 16 * i + 8) & (lane16 < 16 * i + 16),
                               pltpu.roll(v, (16 * i + 8 - 56) % 128, 1), packed)
        s["zp1"][slot] = packed

    def send1(out, slot, base):
        copies = []
        for i, (a, b, c) in enumerate(NEAR):
            rows_src = {-1: (8, 8), 0: (8, 16), 1: (16, 8)}[b]
            rows_dst = {-1: 24, 0: 8, 1: 0}[b]
            if c == 0:
                deep = 5 - slot
                first_plane, count, to = {-1: (5, deep, 13), 0: (5, 8, 5), 1: (13 - deep, deep, 5 - deep)}[a]
                src = out.at[pl.ds(first_plane, count), pl.ds(rows_src[0], rows_src[1])]
                dst = out.at[pl.ds(to, count), pl.ds(rows_dst, rows_src[1])]
            else:
                src = s["zp1"].at[slot, pl.ds(rows_src[0] - 8, rows_src[1])]
                dst = s["zb1"].at[slot, 0 if c == 1 else 1, 1 - a, pl.ds(rows_dst, rows_src[1])]
            copies.append(copy(src, dst, (a, b, c), base + i))
        for c in copies:
            c.start()
        return copies

    def land1(copies, out, slot):
        for c, o in zip(copies, NEAR):
            c.wait_recv()
            if o[2] == 0:
                c.wait_send()
            else:
                sent.append(c)
        for p in range(18):
            x = p - 5
            a = -1 if x < 0 else (0 if x < 8 else 1)
            q = x - 8 * a
            low = pltpu.roll(s["zb1"][slot, 0, a + 1], (120 - 16 * q - 8) % 128, 1)
            high = pltpu.roll(s["zb1"][slot, 1, a + 1], (64 - 16 * q) % 128, 1)
            out[p] = jnp.where(lane32 < 64, out[p],
                               jnp.where(lane32 < 72, high, jnp.where(lane32 >= 120, low, 0.0)))

    def to_level2(plane, first_q, count, slot):
        sums(count, 32, plane)
        rows = pooled_rows(count, 32, 8, 8)
        rows = jnp.where(lanes(rows.shape) < 64, rows, 0.0)
        mean = dot(rows, tab[POOL])
        packs = [jnp.zeros((8, 128), F32), jnp.zeros((8, 128), F32)]
        for i in range(count):
            q = first_q + i
            v = mean[8 * i:8 * i + 8]
            packs[q // 4] = packs[q // 4] + (pltpu.roll(v, 32 * (q % 4), 1) if q % 4 else v)
        s["p2"][slot, 0] = packs[0]
        s["p2"][slot, 1] = packs[1]

    def slot2(a, b, c):
        return 9 * (a + 1) + 3 * (b + 1) + (c + 1)

    def send2(slot, base):
        copies = []
        for i, o in enumerate(NEAR):
            copies.append(copy(s["p2"].at[slot], s["r2"].at[slot, slot2(-o[0], -o[1], -o[2])], o, base + i))
        for c in copies:
            c.start()
        s["r2"][slot, slot2(0, 0, 0)] = s["p2"][slot]
        return copies

    def land2(copies, out, slot):
        arrive(copies)
        for p in range(16):
            x = p - 6
            a = -1 if x < 0 else (0 if x < 4 else 1)
            q = x - 4 * a + 2

            def part(b, c, place):
                v = s["r2"][slot, slot2(a, b, c), q // 4]
                shift = (place - 32 * (q % 4)) % 128
                return pltpu.roll(v, shift, 1) if shift else v
            for b in (-1, 0, 1):
                out[p, 8 * (b + 1):8 * (b + 2), :] = jnp.where(
                    lane8 < 32, part(b, 0, 0),
                    jnp.where(lane8 < 64, part(b, 1, 32), jnp.where(lane8 >= 96, part(b, -1, 96), 0.0)))

    def to_level3(plane, slot):
        for i in range(6):
            v = plane(2 * i) + plane(2 * i + 1)
            total[40 * i:40 * i + 24, :] = v
            total[40 * i + 24:40 * i + 32, :] = v[:8]
            total[40 * i + 32:40 * i + 40, :] = v[:8]
        rows = jnp.concatenate([pooled_rows(6, 40, 4, 8), pooled_rows(6, 40, 20, 8)], axis=0)
        mean = dot(rows, tab[POOL_HALO])
        for i in range(6):
            more = pltpu.roll(mean[48 + 8 * i:56 + 8 * i], 48, 1)
            s["s3"][slot, i] = jnp.where((lane8 >= 32) & (lane8 < 80), more, mean[8 * i:8 * i + 8])

        for i, (p, q) in enumerate(PAIRS):
            s["t3"][slot, i] = jnp.where(
                lane8 < 64, pltpu.roll(s["s3"][slot, p], 16, 1), pltpu.roll(s["s3"][slot, q], 80, 1))

    def send3(slot, base):
        copies = []
        for i, (a, b, c) in enumerate(FAR):
            start, count = {0: (0, 6), 2: (0, 5), -2: (1, 5), 4: (0, 5), -4: (1, 5)}[a]
            if slot == 1 and abs(a) == 4:
                start, count = 1, 4
            if b == 0:
                src = s["s3"].at[slot, pl.ds(start, count)]
                dst = s["r3"].at[slot, 2 - a // 2, pl.ds(start, count)]
            else:
                tiles = pl.ds(1, 2) if count == 4 else pl.ds(0, 3)
                src = s["t3"].at[slot, tiles]
                dst = s["q3"].at[slot, 2 - a // 2, 0 if b == 2 else 1, tiles]
            copies.append(copy(src, dst, (a, b, c), base + i))
        for c in copies:
            c.start()
        s["r3"][slot, 2] = s["s3"][slot]
        return copies

    def land3(copies, out, slot, low, high):
        arrive(copies)
        row8 = lax.broadcasted_iota(jnp.int32, (8, 128), 0)
        edge = {-1: (gy < 2) & (row8 >= 6), 1: (gy >= GY - 2) & (row8 < 2)}
        others = {-6: (-2, gx < 4), -2: (0, gx < 2), 3: (0, gx >= GX - 2), 7: (2, gx >= GX - 4)}
        for p in range(low, high):
            x = p - 10
            a = -4 if x < -5 else -2 if x < -1 else 0 if x < 3 else 2 if x < 7 else 4

            def tile(a, b):
                q = x - 2 * a + 2
                if b == 0:
                    return s["r3"][slot, 2 + a // 2, q]
                i = [q in pair for pair in PAIRS].index(True)
                return pltpu.roll(s["q3"][slot, 2 + a // 2, 0 if b < 0 else 1, i], 112 if q == PAIRS[i][0] else 48, 1)

            def part(b):
                v = tile(a, b)
                if x in others:
                    near, when = others[x]
                    v = jnp.where(when, tile(near, b), v)
                return v
            middle = part(0)
            more = pltpu.roll(middle, 80, 1)
            out[p, 0:8, :] = jnp.where(edge[-1], more, part(-1))
            out[p, 8:16, :] = middle
            out[p, 16:24, :] = jnp.where(edge[1], more, part(1))

    def repeat_rows(value, count, rows, start, keep):
        rep = s["rep"]
        for i in range(count):
            v = value[rows * i + start:rows * i + start + keep]
            rep[pl.ds(2 * keep * i, keep, stride=2), :] = v
            rep[pl.ds(2 * keep * i + 1, keep, stride=2), :] = v

    base1, base2, base3 = 6 * ROUNDS, 6 * ROUNDS + 52, 6 * ROUNDS + 104
    for i, table in enumerate(tables()):
        tab[i] = table
    load_kap.wait()
    pack(s["k0"], 0)
    pl.semaphore_wait(barrier, len(FACES))
    moving0 = faces(s["k0"], 0)
    to_level1(lambda x: s["k0"][1 + x, 8:40, :], s["k1"], 0)
    clear0(s["ua"])
    clear0(s["ub"])
    load_rhs.wait()
    arrive(moving0)
    land(s["k0"], 0, 0)
    row32 = lax.broadcasted_iota(jnp.int32, (32, 128), 0)
    for x in range(16):
        c, others = around0(s["k0"], x)
        end = ends(x, 0)
        others[4] = jnp.where(lane32 == 0, end, others[4])
        others[5] = jnp.where(lane32 == 127, end, others[5])
        w = [0.5 * (c + other) for other in others]
        diag = w[0] + w[1] + w[2] + w[3] + w[4] + w[5]
        s["wz"][x] = jnp.where(lane32 == 0, w[4], jnp.where(lane32 == 127, w[5], 0.0))
        s["wy"][x] = jnp.where(row32 == 0, w[2], jnp.where(row32 == 31, w[3], 0.0))
        w[4] = jnp.where(lane32 == 0, 0.0, w[4])
        w[5] = jnp.where(lane32 == 127, 0.0, w[5])
        for i in range(6):
            s["w0"][i, x] = w[i]
        s["d0"][x] = diag
        inv = OMEGA / diag
        s["i0"][x] = inv
        s["ua"][1 + x, 8:40, :] = rhs[x] * inv

    pack(s["ua"], 1)
    moving0 = faces(s["ua"], 1)
    partial0(s["ua"])
    arrive(moving0)
    merge(1, 0)
    for x in range(16):
        s["ub"][1 + x, 8:40, :] = s["ua"][1 + x, 8:40, :] + s["i0"][x] * finish0(1, x)
    pack(s["ub"], 2)
    moving0 = faces(s["ub"], 2)
    coefficient1 = send1(s["k1"], 0, base1)
    partial0(s["ub"])
    arrive(moving0)
    merge(2, 0)
    for x in range(16):
        residual[x] = finish0(2, x)
    to_level1(lambda x: residual[x], s["f1"], 1)
    moving1 = send1(s["f1"], 1, base1 + 26)
    drain()
    land1(coefficient1, s["k1"], 0)
    to_level2(lambda i: s["k1"][1 + i], 0, 8, 0)
    coefficient2 = send2(0, base2)
    weights(L1, s["k1"], s["w1"], s["d1"], s["i1"])
    land(s["ub"], 2, 1)
    land1(moving1, s["f1"], 1)

    first(s["u1a"], s["f1"], s["i1"], 1, 17)
    sweep(L1, s["u1a"], s["u1b"], s["f1"], s["w1"], s["d1"], s["i1"], 2, 16)

    def rest1(p):
        s["u1a"][p] = rest(L1, s["u1b"], s["f1"], s["w1"], s["d1"], p)[1]
    loop(3, 15, rest1)
    to_level2(lambda i: s["u1a"][3 + i], 1, 6, 1)
    moving2 = send2(1, base2 + 26)
    drain()
    land2(coefficient2, s["k2"], 0)
    to_level3(lambda i: s["k2"][2 + i], 0)
    coefficient3 = send3(0, base3)
    weights(L2, s["k2"], s["w2"], s["d2"], s["i2"])
    land2(moving2, s["f2"], 1)

    first(s["u2a"], s["f2"], s["i2"], 1, 15)
    sweep(L2, s["u2a"], s["u2b"], s["f2"], s["w2"], s["d2"], s["i2"], 2, 14)

    def rest2(p):
        s["u2a"][p] = rest(L2, s["u2b"], s["f2"], s["w2"], s["d2"], p)[1]
    s["u2b"][1] = jnp.zeros((24, 128), F32)
    s["u2b"][14] = jnp.zeros((24, 128), F32)
    loop(2, 14, rest2)
    to_level3(lambda i: s["u2a"][2 + i], 1)
    moving3 = send3(1, base3 + 14)
    drain()
    land3(coefficient3, s["k3"], 0, 0, 22)
    weights(L3, s["k3"], s["w3"], s["d3"], s["i3"])
    land3(moving3, s["f3"], 1, 1, 21)

    u, v = s["u3a"], s["u3b"]
    first(u, s["f3"], s["i3"], 1, 21)
    for step in range(COARSE_SWEEPS - 1):
        sweep(L3, u, v, s["f3"], s["w3"], s["d3"], s["i3"], 2 + step, 20 - step)
        u, v = v, u

    rep = s["rep"]
    value = dot(u[8:14].reshape(6 * 24, 128), tab[REPEAT_64])
    repeat_rows(value, 6, 24, 6, 12)
    for p in range(2, 14):
        i = p // 2 - 1
        s["u2b"][p] = s["u2b"][p] + rep[24 * i:24 * i + 24, :]
    sweep(L2, s["u2b"], s["u2a"], s["f2"], s["w2"], s["d2"], s["i2"], 3, 13)
    sweep(L2, s["u2a"], s["u2b"], s["f2"], s["w2"], s["d2"], s["i2"], 4, 12)

    value = dot(s["u2b"][4:12].reshape(8 * 24, 128), tab[REPEAT_96])
    repeat_rows(value, 8, 24, 4, 16)
    for p in range(2, 16):
        i = (p + 7) // 2 - 4
        s["u1b"][p] = s["u1b"][p] + rep[32 * i:32 * i + 32, :]
    sweep(L1, s["u1b"], s["u1a"], s["f1"], s["w1"], s["d1"], s["i1"], 3, 15)
    sweep(L1, s["u1a"], s["u1b"], s["f1"], s["w1"], s["d1"], s["i1"], 4, 14)

    value = s["u1b"][4:14].reshape(10 * 32, 128)
    repeat_rows(dot(value, tab[EDGES]), 10, 32, 4, 24)
    for x in range(16):
        i = (x + 10) // 2 - 4
        s["h0"][x] = ends(x, 1) + rep[48 * i + 8:48 * i + 40, :]
    repeat_rows(dot(value, tab[REPEAT_128]), 10, 32, 4, 24)
    for p in range(18):
        i = (p + 9) // 2 - 4
        if p in (0, 17):
            s["ub"][p, 8:40, :] = s["ub"][p, 8:40, :] + rep[48 * i + 8:48 * i + 40, :]
        else:
            s["ub"][p, 7:41, :] = s["ub"][p, 7:41, :] + rep[48 * i + 7:48 * i + 41, :]

    for x in range(16):
        c, acc = core0(s["ub"], x)
        s["ua"][1 + x, 8:40, :] = c + s["i0"][x] * (acc + s["wz"][x] * s["h0"][x])
    pack(s["ua"], 3)
    moving0 = faces(s["ua"], 3)
    partial0(s["ua"])
    clear0(s["ub"])
    arrive(moving0)
    merge(3, 0)
    for x in range(16):
        s["ub"][1 + x, 8:40, :] = s["ua"][1 + x, 8:40, :] + s["i0"][x] * finish0(3, x)
    pack(s["ub"], 4)
    moving0 = faces(s["ub"], 4)
    partial0(s["ub"])
    for x in range(16):
        pressure[x] = s["ub"][1 + x, 8:40, :]
    arrive(moving0)
    merge(4, 0)
    for x in range(16):
        residual[x] = finish0(4, x)
    drain()


def cycle(rhs, kappa):
    block = jax.ShapeDtypeStruct((16, 32, 128), F32)
    vmem = pl.BlockSpec(memory_space=pltpu.VMEM)
    return pl.pallas_call(
        kernel,
        out_shape=(block, block),
        in_specs=[pl.BlockSpec(memory_space=pltpu.HBM)] * 2,
        out_specs=(vmem, vmem),
        scratch_shapes=[pltpu.VMEM(shape, F32) for shape in SCRATCH.values()] + [
            pltpu.SemaphoreType.DMA((COPIES,)), pltpu.SemaphoreType.DMA((COPIES,)),
            pltpu.SemaphoreType.DMA((2,)), pltpu.VMEM((6, 128, 128), BF16)],
        compiler_params=pltpu.CompilerParams(
            collective_id=0, has_side_effects=True, vmem_limit_bytes=40 * 1024 * 1024),
        cost_estimate=pl.CostEstimate(flops=40_000_000, bytes_accessed=1_048_576, transcendentals=0),
    )(rhs, kappa)


def solution(mesh):
    placed = (P("gx", "gy", "gz"), P("gx", "gy", "gz"))
    return jax.shard_map(
        cycle, mesh=mesh, in_specs=placed, out_specs=(P("gx", "gy", "gz"), P("gx", "gy", "gz")), check_vma=False)
```

```python
import functools
import itertools

import jax
import jax.numpy as jnp
from jax import lax
from jax.experimental import pallas as pl
from jax.experimental.pallas import tpu as pltpu
from jax.sharding import PartitionSpec as P

MESH = pl.DeviceIdType.MESH
F32 = jnp.float32
BF16 = jnp.bfloat16
OMEGA = 0.8
COARSE_SWEEPS = 8
GX, GY, GZ = 16, 8, 4
FACES = [(-1, 0, 0), (1, 0, 0), (0, -1, 0), (0, 1, 0), (0, 0, -1), (0, 0, 1)]
NEAR = sorted((o for o in itertools.product((-1, 0, 1), repeat=3) if o != (0, 0, 0)), key=lambda o: -sum(map(abs, o)))
FAR = sorted(((a, b, 0) for a in (-4, -2, 0, 2, 4) for b in (-2, 0, 2) if (a, b) != (0, 0)),
             key=lambda o: -sum(map(abs, o)))
ROUNDS = 5
PAIRS = [(0, 5), (1, 2), (3, 4)]

L1 = dict(planes=18, rows=32, px=5, py=8, n=(8, 16, 64), right=72, left=120, level=1)
L2 = dict(planes=16, rows=24, px=6, py=8, n=(4, 8, 32), right=64, left=96, level=2)
L3 = dict(planes=22, rows=24, px=10, py=10, n=(2, 4, 16), right=32, left=112, level=3)

SCRATCH = {
    "ua": (18, 48, 128), "ub": (18, 48, 128), "k0": (18, 48, 128),
    "f0": (16, 32, 128), "part": (16, 32, 128), "wy": (16, 32, 128), "wz": (16, 32, 128), "w0": (6, 16, 32, 128), "d0": (16, 32, 128), "i0": (16, 32, 128), "h0": (16, 32, 128),
    "ys": (ROUNDS, 2, 16, 128), "zs": (ROUNDS, 8, 128),
    "rx": (ROUNDS, 2, 32, 128), "ry": (ROUNDS, 2, 16, 128), "rz": (ROUNDS, 2, 8, 128), "mz": (2, 8, 128),
    "sum": (256, 128), "rep": (10 * 48, 128),
    "k1": (18, 32, 128), "f1": (18, 32, 128), "u1a": (18, 32, 128), "u1b": (18, 32, 128),
    "w1": (6, 18, 32, 128), "d1": (18, 32, 128), "i1": (18, 32, 128),
    "zp1": (2, 16, 128), "zb1": (2, 2, 3, 32, 128),
    "k2": (16, 24, 128), "f2": (16, 24, 128), "u2a": (16, 24, 128), "u2b": (16, 24, 128),
    "w2": (6, 16, 24, 128), "d2": (16, 24, 128), "i2": (16, 24, 128),
    "p2": (2, 2, 8, 128), "r2": (2, 27, 2, 8, 128),
    "k3": (22, 24, 128), "f3": (22, 24, 128), "u3a": (22, 24, 128), "u3b": (22, 24, 128),
    "w3": (6, 22, 24, 128), "d3": (22, 24, 128), "i3": (22, 24, 128),
    "s3": (2, 6, 8, 128), "t3": (2, 3, 8, 128), "r3": (2, 5, 6, 8, 128), "q3": (2, 5, 2, 3, 8, 128),
}
COPIES = ROUNDS * 6 + 2 * (26 + 26 + 14)


def lanes(shape):
    return lax.broadcasted_iota(jnp.int32, shape, len(shape) - 1)


def loop(low, high, body):
    def step(i, carry):
        body(i)
        return carry
    lax.fori_loop(low, high, step, 0, unroll=True)


def dot(a, b):
    high = a.astype(BF16)
    low = (a - high.astype(F32)).astype(BF16)
    return (jnp.dot(high, b, preferred_element_type=F32) + jnp.dot(low, b, preferred_element_type=F32))


def tables():
    row = lax.broadcasted_iota(jnp.int32, (128, 128), 0)
    col = lax.broadcasted_iota(jnp.int32, (128, 128), 1)

    def half(index, split):
        return jnp.where(index < split, index // 2, 64 + index // 2)
    pools = [jnp.where(half(row, split) == col, 0.125, 0.0) for split in (128, 64)]
    repeats = [jnp.where(half(col, split) == row, 1.0, 0.0) for split in (64, 96, 128)]
    edges = jnp.where(((row == 127) & (col == 0)) | ((row == 64) & (col == 127)), 1.0, 0.0)
    return [m.astype(BF16) for m in pools + repeats + [edges]]


POOL, POOL_HALO, REPEAT_64, REPEAT_96, REPEAT_128, EDGES = range(6)


def kernel(rhs_in, kap_in, pressure, residual, *refs):
    s = dict(zip(SCRATCH, refs))
    send, recv, load, tab = refs[len(SCRATCH):]
    rhs = s["f0"]
    gx, gy, gz = lax.axis_index("gx"), lax.axis_index("gy"), lax.axis_index("gz")

    at_x = {a: (gx + a) & (GX - 1) for a in (-4, -2, -1, 1, 2, 4)} | {0: gx}
    at_y = {a: (gy + a) & (GY - 1) for a in (-2, -1, 1, 2)} | {0: gy}
    at_z = {a: (gz + a) & (GZ - 1) for a in (-1, 1)} | {0: gz}
    sent = []

    def device(o):
        return (at_x[o[0]], at_y[o[1]], at_z[o[2]])

    def drain():
        for c in sent:
            c.wait_send()
        sent.clear()

    def copy(src, dst, o, index):
        return pltpu.make_async_remote_copy(
            src_ref=src, dst_ref=dst, send_sem=send.at[index], recv_sem=recv.at[index],
            device_id=device(o), device_id_type=MESH)

    barrier = pltpu.get_barrier_semaphore()
    for o in FACES:
        pl.semaphore_signal(barrier, inc=1, device_id=device(o), device_id_type=MESH)
    load_kap = pltpu.make_async_copy(kap_in, s["k0"].at[pl.ds(1, 16), pl.ds(8, 32)], load.at[0])
    load_rhs = pltpu.make_async_copy(rhs_in, rhs, load.at[1])
    load_kap.start()
    load_rhs.start()

    lane8 = lanes((8, 128))
    lane32 = lanes((32, 128))
    total = s["sum"]

    def pack(u, r):
        for x in range(16):
            s["ys"][r, 0, x:x + 1, :] = u[1 + x, 8:9, :]
            s["ys"][r, 1, x:x + 1, :] = u[1 + x, 39:40, :]
        packed = jnp.zeros((8, 128), F32)
        for x in range(16):
            for t in range(4):
                k = 4 * x + t
                moved = pltpu.roll(u[1 + x, 8 + 8 * t:16 + 8 * t, :], (2 * k + 1) % 128, 1)
                packed = jnp.where((lane8 >> 1) == k, moved, packed)
        s["zs"][r] = packed

    def faces(u, r):
        base = 6 * r
        copies = []
        for i, o in enumerate(FACES):
            low = i % 2 == 0
            side = 1 if low else 0
            if i < 2:
                src, dst = u.at[1 if low else 16, pl.ds(8, 32)], s["rx"].at[r, side]
            elif i < 4:
                src, dst = s["ys"].at[r, 0 if low else 1], s["ry"].at[r, side]
            else:
                src, dst = s["zs"].at[r], s["rz"].at[r, side]
            copies.append(copy(src, dst, o, base + i))
        for c in copies:
            c.start()
        drain()
        return copies

    def arrive(copies):
        for c in copies:
            c.wait_recv()
        sent.extend(copies)

    def land(u, r, out):
        u[0, 8:40, :] = jnp.where(gx > 0, s["rx"][r, 0], 0.0)
        u[17, 8:40, :] = jnp.where(gx < GX - 1, s["rx"][r, 1], 0.0)
        below = jnp.where(gy > 0, s["ry"][r, 0], 0.0)
        above = jnp.where(gy < GY - 1, s["ry"][r, 1], 0.0)
        for x in range(16):
            u[1 + x, 7:8, :] = below[x:x + 1]
            u[1 + x, 40:41, :] = above[x:x + 1]
        merge(r, out)

    def merge(r, out):
        left = jnp.where(gz > 0, s["rz"][r, 0], 0.0)
        right = jnp.where(gz < GZ - 1, s["rz"][r, 1], 0.0)
        s["mz"][out] = jnp.where((lane8 & 1) == 0, left, pltpu.roll(right, 126, 1))

    def ends(x, at):
        packed = s["mz"][at]
        return jnp.concatenate(
            [pltpu.roll(packed, (-8 * x - 2 * t) % 128, 1) if x + t else packed for t in range(4)], axis=0)

    def around0(u, x):
        c = u[1 + x, 8:40, :]
        return c, [u[x, 8:40, :], u[2 + x, 8:40, :], u[1 + x, 7:39, :], u[1 + x, 9:41, :],
                   pltpu.roll(c, 1, 1), pltpu.roll(c, 127, 1)]

    def core0(u, x):
        c, others = around0(u, x)
        acc = rhs[x] - s["d0"][x] * c
        for i in range(6):
            acc = acc + s["w0"][i, x] * others[i]
        return c, acc

    def partial0(u):
        for x in range(16):
            s["part"][x] = core0(u, x)[1]

    def finish0(r, x):
        acc = s["part"][x] + s["wz"][x] * ends(x, 0)
        if x == 0:
            acc = acc + s["w0"][0, 0] * jnp.where(gx > 0, s["rx"][r, 0], 0.0)
        if x == 15:
            acc = acc + s["w0"][1, 15] * jnp.where(gx < GX - 1, s["rx"][r, 1], 0.0)
        below = jnp.broadcast_to(jnp.where(gy > 0, s["ry"][r, 0, x:x + 1, :], 0.0), (8, 128))
        above = jnp.broadcast_to(jnp.where(gy < GY - 1, s["ry"][r, 1, x:x + 1, :], 0.0), (8, 128))
        return jnp.concatenate(
            [acc[:8] + s["wy"][x, :8] * below, acc[8:24], acc[24:] + s["wy"][x, 24:] * above], axis=0)

    def clear0(u):
        u[0] = jnp.zeros((48, 128), F32)
        u[17] = jnp.zeros((48, 128), F32)
        for x in range(16):
            u[1 + x, 0:8, :] = jnp.zeros((8, 128), F32)
            u[1 + x, 40:48, :] = jnp.zeros((8, 128), F32)

    def inside(lv, p):
        n, level = lv["n"], lv["level"]
        shape = (lv["rows"], 128)
        lane = lanes(shape)
        row = lax.broadcasted_iota(jnp.int32, shape, 0)
        x = gx * n[0] + (p - lv["px"])
        y = gy * n[1] + (row - lv["py"])
        z = gz * n[2] + jnp.where(lane < lv["right"], lane, lane - 128)
        ok = (lane < lv["right"]) | (lane >= lv["left"])
        ok = ok & (y >= 0) & (y < 256 >> level) & (z >= 0) & (z < 512 >> level)
        return ok & (x >= 0) & (x < 256 >> level)

    def around(u, p, rows):
        c = u[p]
        return c, [u[p - 1], u[p + 1], pltpu.roll(c, 1, 0), pltpu.roll(c, rows - 1, 0),
                   pltpu.roll(c, 1, 1), pltpu.roll(c, 127, 1)]

    def weights(lv, k, w, d, inv):
        scale = 0.5 * 0.25 ** lv["level"]

        def clear(p):
            k[p] = jnp.where(inside(lv, p), k[p], 0.0)

        row = lax.broadcasted_iota(jnp.int32, (lv["rows"], 128), 0)
        ends_y = {2: row == 0, 3: row == lv["rows"] - 1}

        def plane(p):
            c, others = around(k, p, lv["rows"])
            diag = None
            for i in range(6):
                other = jnp.where(ends_y[i], 0.0, others[i]) if i in ends_y else others[i]
                weight = scale * (c + other)
                w[i, p] = jnp.where(ends_y[i], 0.0, weight) if i in ends_y else weight
                diag = weight if diag is None else diag + weight
            d[p] = diag
            inv[p] = jnp.where(inside(lv, p), OMEGA / diag, 0.0)
        loop(0, lv["planes"], clear)
        loop(1, lv["planes"] - 1, plane)

    def rest(lv, u, f, w, d, p):
        c, others = around(u, p, lv["rows"])
        acc = f[p] - d[p] * c
        for i in range(6):
            acc = acc + w[i, p] * others[i]
        return c, acc

    def sweep(lv, u, v, f, w, d, inv, low, high):
        def plane(p):
            c, others = around(u, p, lv["rows"])
            acc = f[p]
            for i in range(6):
                acc = acc + w[i, p] * others[i]
            v[p] = (1.0 - OMEGA) * c + inv[p] * acc
        loop(low, high, plane)

    def first(u, f, inv, low, high):
        def plane(p):
            u[p] = f[p] * inv[p]
        loop(low, high, plane)

    def pooled_rows(count, rows, start, keep):
        parts = []
        for i in range(count):
            parts.append(total[pl.ds(rows * i + start, keep, stride=2), :]
                         + total[pl.ds(rows * i + start + 1, keep, stride=2), :])
        return jnp.concatenate(parts, axis=0)

    def sums(count, rows, plane):
        for i in range(count):
            total[rows * i:rows * i + rows, :] = plane(2 * i) + plane(2 * i + 1)

    def to_level1(plane, out, slot):
        sums(8, 32, plane)
        mean = dot(pooled_rows(8, 32, 0, 16), tab[POOL])
        for i in range(8):
            out[5 + i, 8:24, :] = mean[16 * i:16 * i + 16]
        lane16 = lanes((16, 128))
        packed = jnp.zeros((16, 128), F32)
        for i in range(8):
            v = mean[16 * i:16 * i + 16]
            packed = jnp.where((lane16 >= 16 * i) & (lane16 < 16 * i + 8), pltpu.roll(v, 16 * i, 1) if i else v, packed)
            packed = jnp.where((lane16 >= 16 * i + 8) & (lane16 < 16 * i + 16),
                               pltpu.roll(v, (16 * i + 8 - 56) % 128, 1), packed)
        s["zp1"][slot] = packed

    def send1(out, slot, base):
        copies = []
        for i, (a, b, c) in enumerate(NEAR):
            rows_src = {-1: (8, 8), 0: (8, 16), 1: (16, 8)}[b]
            rows_dst = {-1: 24, 0: 8, 1: 0}[b]
            if c == 0:
                deep = 5 - slot
                first_plane, count, to = {-1: (5, deep, 13), 0: (5, 8, 5), 1: (13 - deep, deep, 5 - deep)}[a]
                src = out.at[pl.ds(first_plane, count), pl.ds(rows_src[0], rows_src[1])]
                dst = out.at[pl.ds(to, count), pl.ds(rows_dst, rows_src[1])]
            else:
                src = s["zp1"].at[slot, pl.ds(rows_src[0] - 8, rows_src[1])]
                dst = s["zb1"].at[slot, 0 if c == 1 else 1, 1 - a, pl.ds(rows_dst, rows_src[1])]
            copies.append(copy(src, dst, (a, b, c), base + i))
        for c, o in sorted(zip(copies, NEAR), key=lambda e: e[1][2] != 0):
            c.start()
        return copies

    def land1(copies, out, slot):
        for c, o in zip(copies, NEAR):
            c.wait_recv()
            if o[2] == 0:
                c.wait_send()
            else:
                sent.append(c)
        for p in range(18):
            x = p - 5
            a = -1 if x < 0 else (0 if x < 8 else 1)
            q = x - 8 * a
            low = pltpu.roll(s["zb1"][slot, 0, a + 1], (120 - 16 * q - 8) % 128, 1)
            high = pltpu.roll(s["zb1"][slot, 1, a + 1], (64 - 16 * q) % 128, 1)
            out[p] = jnp.where(lane32 < 64, out[p],
                               jnp.where(lane32 < 72, high, jnp.where(lane32 >= 120, low, 0.0)))

    def to_level2(plane, first_q, count, slot):
        sums(count, 32, plane)
        rows = pooled_rows(count, 32, 8, 8)
        rows = jnp.where(lanes(rows.shape) < 64, rows, 0.0)
        mean = dot(rows, tab[POOL])
        packs = [jnp.zeros((8, 128), F32), jnp.zeros((8, 128), F32)]
        for i in range(count):
            q = first_q + i
            v = mean[8 * i:8 * i + 8]
            packs[q // 4] = packs[q // 4] + (pltpu.roll(v, 32 * (q % 4), 1) if q % 4 else v)
        s["p2"][slot, 0] = packs[0]
        s["p2"][slot, 1] = packs[1]

    def slot2(a, b, c):
        return 9 * (a + 1) + 3 * (b + 1) + (c + 1)

    def send2(slot, base):
        copies = []
        for i, o in enumerate(NEAR):
            copies.append(copy(s["p2"].at[slot], s["r2"].at[slot, slot2(-o[0], -o[1], -o[2])], o, base + i))
        for c in copies:
            c.start()
        s["r2"][slot, slot2(0, 0, 0)] = s["p2"][slot]
        return copies

    def land2(copies, out, slot):
        arrive(copies)
        for p in range(16):
            x = p - 6
            a = -1 if x < 0 else (0 if x < 4 else 1)
            q = x - 4 * a + 2

            def part(b, c, place):
                v = s["r2"][slot, slot2(a, b, c), q // 4]
                shift = (place - 32 * (q % 4)) % 128
                return pltpu.roll(v, shift, 1) if shift else v
            for b in (-1, 0, 1):
                out[p, 8 * (b + 1):8 * (b + 2), :] = jnp.where(
                    lane8 < 32, part(b, 0, 0),
                    jnp.where(lane8 < 64, part(b, 1, 32), jnp.where(lane8 >= 96, part(b, -1, 96), 0.0)))

    def to_level3(plane, slot):
        for i in range(6):
            v = plane(2 * i) + plane(2 * i + 1)
            total[40 * i:40 * i + 24, :] = v
            total[40 * i + 24:40 * i + 32, :] = v[:8]
            total[40 * i + 32:40 * i + 40, :] = v[:8]
        rows = jnp.concatenate([pooled_rows(6, 40, 4, 8), pooled_rows(6, 40, 20, 8)], axis=0)
        mean = dot(rows, tab[POOL_HALO])
        for i in range(6):
            more = pltpu.roll(mean[48 + 8 * i:56 + 8 * i], 48, 1)
            s["s3"][slot, i] = jnp.where((lane8 >= 32) & (lane8 < 80), more, mean[8 * i:8 * i + 8])

        for i, (p, q) in enumerate(PAIRS):
            s["t3"][slot, i] = jnp.where(
                lane8 < 64, pltpu.roll(s["s3"][slot, p], 16, 1), pltpu.roll(s["s3"][slot, q], 80, 1))

    def send3(slot, base):
        copies = []
        for i, (a, b, c) in enumerate(FAR):
            start, count = {0: (0, 6), 2: (0, 5), -2: (1, 5), 4: (0, 5), -4: (1, 5)}[a]
            if slot == 1 and abs(a) == 4:
                start, count = 1, 4
            if b == 0:
                src = s["s3"].at[slot, pl.ds(start, count)]
                dst = s["r3"].at[slot, 2 - a // 2, pl.ds(start, count)]
            else:
                tiles = pl.ds(1, 2) if count == 4 else pl.ds(0, 3)
                src = s["t3"].at[slot, tiles]
                dst = s["q3"].at[slot, 2 - a // 2, 0 if b == 2 else 1, tiles]
            copies.append(copy(src, dst, (a, b, c), base + i))
        for c in copies:
            c.start()
        s["r3"][slot, 2] = s["s3"][slot]
        return copies

    def land3(copies, out, slot, low, high):
        arrive(copies)
        row8 = lax.broadcasted_iota(jnp.int32, (8, 128), 0)
        edge = {-1: (gy < 2) & (row8 >= 6), 1: (gy >= GY - 2) & (row8 < 2)}
        others = {-6: (-2, gx < 4), -2: (0, gx < 2), 3: (0, gx >= GX - 2), 7: (2, gx >= GX - 4)}
        for p in range(low, high):
            x = p - 10
            a = -4 if x < -5 else -2 if x < -1 else 0 if x < 3 else 2 if x < 7 else 4

            def tile(a, b):
                q = x - 2 * a + 2
                if b == 0:
                    return s["r3"][slot, 2 + a // 2, q]
                i = [q in pair for pair in PAIRS].index(True)
                return pltpu.roll(s["q3"][slot, 2 + a // 2, 0 if b < 0 else 1, i], 112 if q == PAIRS[i][0] else 48, 1)

            def part(b):
                v = tile(a, b)
                if x in others:
                    near, when = others[x]
                    v = jnp.where(when, tile(near, b), v)
                return v
            middle = part(0)
            more = pltpu.roll(middle, 80, 1)
            out[p, 0:8, :] = jnp.where(edge[-1], more, part(-1))
            out[p, 8:16, :] = middle
            out[p, 16:24, :] = jnp.where(edge[1], more, part(1))

    def repeat_rows(value, count, rows, start, keep):
        rep = s["rep"]
        for i in range(count):
            v = value[rows * i + start:rows * i + start + keep]
            rep[pl.ds(2 * keep * i, keep, stride=2), :] = v
            rep[pl.ds(2 * keep * i + 1, keep, stride=2), :] = v

    base1, base2, base3 = 6 * ROUNDS, 6 * ROUNDS + 52, 6 * ROUNDS + 104
    for i, table in enumerate(tables()):
        tab[i] = table
    load_kap.wait()
    pack(s["k0"], 0)
    pl.semaphore_wait(barrier, len(FACES))
    moving0 = faces(s["k0"], 0)
    to_level1(lambda x: s["k0"][1 + x, 8:40, :], s["k1"], 0)
    clear0(s["ua"])
    clear0(s["ub"])
    load_rhs.wait()
    arrive(moving0)
    land(s["k0"], 0, 0)
    row32 = lax.broadcasted_iota(jnp.int32, (32, 128), 0)
    for x in range(16):
        c, others = around0(s["k0"], x)
        end = ends(x, 0)
        others[4] = jnp.where(lane32 == 0, end, others[4])
        others[5] = jnp.where(lane32 == 127, end, others[5])
        w = [0.5 * (c + other) for other in others]
        diag = w[0] + w[1] + w[2] + w[3] + w[4] + w[5]
        s["wz"][x] = jnp.where(lane32 == 0, w[4], jnp.where(lane32 == 127, w[5], 0.0))
        s["wy"][x] = jnp.where(row32 == 0, w[2], jnp.where(row32 == 31, w[3], 0.0))
        w[4] = jnp.where(lane32 == 0, 0.0, w[4])
        w[5] = jnp.where(lane32 == 127, 0.0, w[5])
        for i in range(6):
            s["w0"][i, x] = w[i]
        s["d0"][x] = diag
        inv = OMEGA / diag
        s["i0"][x] = inv
        s["ua"][1 + x, 8:40, :] = rhs[x] * inv

    pack(s["ua"], 1)
    moving0 = faces(s["ua"], 1)
    partial0(s["ua"])
    arrive(moving0)
    merge(1, 0)
    for x in range(16):
        s["ub"][1 + x, 8:40, :] = s["ua"][1 + x, 8:40, :] + s["i0"][x] * finish0(1, x)
    pack(s["ub"], 2)
    moving0 = faces(s["ub"], 2)
    coefficient1 = send1(s["k1"], 0, base1)
    partial0(s["ub"])
    arrive(moving0)
    merge(2, 0)
    for x in range(16):
        residual[x] = finish0(2, x)
    to_level1(lambda x: residual[x], s["f1"], 1)
    moving1 = send1(s["f1"], 1, base1 + 26)
    drain()
    land1(coefficient1, s["k1"], 0)
    to_level2(lambda i: s["k1"][1 + i], 0, 8, 0)
    coefficient2 = send2(0, base2)
    weights(L1, s["k1"], s["w1"], s["d1"], s["i1"])
    land(s["ub"], 2, 1)
    land1(moving1, s["f1"], 1)

    first(s["u1a"], s["f1"], s["i1"], 1, 17)
    sweep(L1, s["u1a"], s["u1b"], s["f1"], s["w1"], s["d1"], s["i1"], 2, 16)

    def rest1(p):
        s["u1a"][p] = rest(L1, s["u1b"], s["f1"], s["w1"], s["d1"], p)[1]
    loop(3, 15, rest1)
    to_level2(lambda i: s["u1a"][3 + i], 1, 6, 1)
    moving2 = send2(1, base2 + 26)
    drain()
    land2(coefficient2, s["k2"], 0)
    to_level3(lambda i: s["k2"][2 + i], 0)
    coefficient3 = send3(0, base3)
    weights(L2, s["k2"], s["w2"], s["d2"], s["i2"])
    land2(moving2, s["f2"], 1)

    first(s["u2a"], s["f2"], s["i2"], 1, 15)
    sweep(L2, s["u2a"], s["u2b"], s["f2"], s["w2"], s["d2"], s["i2"], 2, 14)

    def rest2(p):
        s["u2a"][p] = rest(L2, s["u2b"], s["f2"], s["w2"], s["d2"], p)[1]
    s["u2b"][1] = jnp.zeros((24, 128), F32)
    s["u2b"][14] = jnp.zeros((24, 128), F32)
    loop(2, 14, rest2)
    to_level3(lambda i: s["u2a"][2 + i], 1)
    moving3 = send3(1, base3 + 14)
    drain()
    land3(coefficient3, s["k3"], 0, 0, 22)
    weights(L3, s["k3"], s["w3"], s["d3"], s["i3"])
    land3(moving3, s["f3"], 1, 1, 21)

    u, v = s["u3a"], s["u3b"]
    first(u, s["f3"], s["i3"], 1, 21)
    for step in range(COARSE_SWEEPS - 1):
        sweep(L3, u, v, s["f3"], s["w3"], s["d3"], s["i3"], 2 + step, 20 - step)
        u, v = v, u

    rep = s["rep"]
    value = dot(u[8:14].reshape(6 * 24, 128), tab[REPEAT_64])
    repeat_rows(value, 6, 24, 6, 12)
    for p in range(2, 14):
        i = p // 2 - 1
        s["u2b"][p] = s["u2b"][p] + rep[24 * i:24 * i + 24, :]
    sweep(L2, s["u2b"], s["u2a"], s["f2"], s["w2"], s["d2"], s["i2"], 3, 13)
    sweep(L2, s["u2a"], s["u2b"], s["f2"], s["w2"], s["d2"], s["i2"], 4, 12)

    value = dot(s["u2b"][4:12].reshape(8 * 24, 128), tab[REPEAT_96])
    repeat_rows(value, 8, 24, 4, 16)
    for p in range(2, 16):
        i = (p + 7) // 2 - 4
        s["u1b"][p] = s["u1b"][p] + rep[32 * i:32 * i + 32, :]
    sweep(L1, s["u1b"], s["u1a"], s["f1"], s["w1"], s["d1"], s["i1"], 3, 15)
    sweep(L1, s["u1a"], s["u1b"], s["f1"], s["w1"], s["d1"], s["i1"], 4, 14)

    value = s["u1b"][4:14].reshape(10 * 32, 128)
    repeat_rows(dot(value, tab[EDGES]), 10, 32, 4, 24)
    for x in range(16):
        i = (x + 10) // 2 - 4
        s["h0"][x] = ends(x, 1) + rep[48 * i + 8:48 * i + 40, :]
    repeat_rows(dot(value, tab[REPEAT_128]), 10, 32, 4, 24)
    for p in range(18):
        i = (p + 9) // 2 - 4
        if p in (0, 17):
            s["ub"][p, 8:40, :] = s["ub"][p, 8:40, :] + rep[48 * i + 8:48 * i + 40, :]
        else:
            s["ub"][p, 7:41, :] = s["ub"][p, 7:41, :] + rep[48 * i + 7:48 * i + 41, :]

    for x in range(16):
        c, acc = core0(s["ub"], x)
        s["ua"][1 + x, 8:40, :] = c + s["i0"][x] * (acc + s["wz"][x] * s["h0"][x])
    pack(s["ua"], 3)
    moving0 = faces(s["ua"], 3)
    partial0(s["ua"])
    clear0(s["ub"])
    arrive(moving0)
    merge(3, 0)
    for x in range(16):
        s["ub"][1 + x, 8:40, :] = s["ua"][1 + x, 8:40, :] + s["i0"][x] * finish0(3, x)
    pack(s["ub"], 4)
    moving0 = faces(s["ub"], 4)
    partial0(s["ub"])
    for x in range(16):
        pressure[x] = s["ub"][1 + x, 8:40, :]
    arrive(moving0)
    merge(4, 0)
    for x in range(16):
        residual[x] = finish0(4, x)
    drain()


def cycle(rhs, kappa):
    block = jax.ShapeDtypeStruct((16, 32, 128), F32)
    vmem = pl.BlockSpec(memory_space=pltpu.VMEM)
    return pl.pallas_call(
        kernel,
        out_shape=(block, block),
        in_specs=[pl.BlockSpec(memory_space=pltpu.HBM)] * 2,
        out_specs=(vmem, vmem),
        scratch_shapes=[pltpu.VMEM(shape, F32) for shape in SCRATCH.values()] + [
            pltpu.SemaphoreType.DMA((COPIES,)), pltpu.SemaphoreType.DMA((COPIES,)),
            pltpu.SemaphoreType.DMA((2,)), pltpu.VMEM((6, 128, 128), BF16)],
        compiler_params=pltpu.CompilerParams(
            collective_id=0, has_side_effects=True, vmem_limit_bytes=40 * 1024 * 1024),
        cost_estimate=pl.CostEstimate(flops=40_000_000, bytes_accessed=1_048_576, transcendentals=0),
    )(rhs, kappa)


def solution(mesh):
    placed = (P("gx", "gy", "gz"), P("gx", "gy", "gz"))
    return jax.shard_map(
        cycle, mesh=mesh, in_specs=placed, out_specs=(P("gx", "gy", "gz"), P("gx", "gy", "gz")), check_vma=False)
```
